32 devices in a mesh: expert: 4 (over z), tensor: 4 (over y, x), dp: 2 (over core).
Axes of the slice: x: 2, y: 2, z: 4, core: 2. Of those that a mesh axis runs over, the one named last changes fastest.
Arguments:
- images: bfloat16 [24, 197, 768], P(('expert', 'dp')), may hold values from -6 to 6
- cotangent: bfloat16 [24, 197, 768], P(('expert', 'dp')), may hold values from -6 to 6
- image_count: int32 [8], P(('expert', 'dp')), may hold values from 2 to 3
- expert_ids: int32 [24, 197, 2], P(('expert', 'dp')), may hold values from 0 to 3, all different within a row; in each aligned block of 591 rows (0 to 590, 591 to 1181, ..., all dimensions but the last counted through in order) at most 304 rows name the same one
- ln1_gain: float32 [768], replicated, may hold values from 0.5 to 1.5
- qkv_weight: bfloat16 [768, 2304], P(None, 'tensor'), may hold values from -0.21875 to 0.21875
- proj_weight: bfloat16 [768, 768], P('tensor'), may hold values from -0.8984375 to 0.8984375
- ln2_gain: float32 [768], replicated, may hold values from 0.5 to 1.5
- router_weight: bfloat16 [768, 4], replicated, may hold values from -0.14941406 to 0.14941406
- expert_up: bfloat16 [4, 768, 3072], P('expert', None, 'tensor'), may hold values from -0.21875 to 0.21875
- expert_down: bfloat16 [4, 3072, 768], P('expert', 'tensor'), may hold values from -1.6953125 to 1.6953125
Outputs:
- block_output: bfloat16 [24, 197, 768], P(('expert', 'dp'))
- input_grad: float32 [24, 197, 768], P(('expert', 'dp'))
- ln1_gain_grad: float32 [768], replicated
- qkv_grad: float32 [768, 2304], P(None, 'tensor')
- proj_grad: float32 [768, 768], P('tensor')
- ln2_gain_grad: float32 [768], replicated
- router_grad: float32 [768, 4], replicated
- up_grad: float32 [4, 768, 3072], P('expert', None, 'tensor')
- down_grad: float32 [4, 3072, 768], P('expert', 'tensor')
The draws below stay inside these ranges and needn't reach their ends.
Inputs may be any that keep to these rules, and one draw needn't show every extreme that they name: `expert_ids`: each token names two different experts. Among the 591 tokens of one group each expert is named by at most 304 rows, and by exactly 304 rows in some group. `image_count`: the number of a group's 3 image slots, from the first, that hold real images; the other slots are padding.
All inputs are finite; a program needn't handle non-finite values.
Results may differ from the reference program's by a relative error of at most 0.018.
Values may be sent and summed in bfloat16 or wider, within the bound.
No kernel may reach another device: no remote copies, remote signals or barrier semaphores. Data moves between devices by JAX's collectives and lax.ppermute only.
A program may use at most 128 MiB of HBM per device.

```python
import math
import jax
import jax.numpy as jnp
import numpy as np
from jax import lax

D = 768
HEADS = 12
HD = 64
FF = 3072
S = 197
IMG_DEV = 3
EXPERTS = 4
TOK_DEV = 591
GROUPS = 8
IMAGES = 24
CAP = 304


def place_ends(values, stream_key, low, top_value):
    dims = values.shape
    place = [jax.random.randint(jax.random.fold_in(stream_key, axis), (), 0, dims[axis]) for axis in range(len(dims))]
    values = values.at[tuple(place)].set(low)
    longest = dims.index(max(dims))
    place[longest] = (place[longest] + 1) % dims[longest]
    return values.at[tuple(place)].set(top_value)


def levels(own_key, extent, shards, smallest, high):
    gain, own = 1.0, jax.random.fold_in(own_key, 6)
    for dim, shards_of in shards:
        steps = jnp.exp(jax.random.uniform(jax.random.fold_in(own, dim), (shards_of,), jnp.float32, smallest / len(shards), high / len(shards)))
        gain = gain * jnp.repeat(steps, extent[dim] // shards_of).reshape([-1 if axis == dim else 1 for axis in range(len(extent))])
    return gain


def deal_out(key, own, number, rows, count, top, limit, lean):
    sequence = jax.random.permutation(key, count)
    packed, usual = load_shares(count, rows * top, limit, lean, True), load_shares(count, rows * top, limit, lean, False)
    places = jnp.arange(count)

    def named(tallies, rotation):
        used = int((tallies > 0).sum())
        fixed = max(1, used // 4)
        passed = fixed + (places - fixed + rotation * (used - fixed)) % max(1, count - fixed)
        return jnp.zeros((count,), jnp.int32).at[sequence[jnp.where(places < fixed, places, passed)]].set(jnp.asarray(tallies, jnp.int32))

    tallies = jnp.where(number % 4 == 0, named(packed, number // 4), named(usual, number - number // 4 - 1))
    mixed = jax.random.permutation(jax.random.fold_in(own, 3), count)
    donor, sink = mixed[0:count // 2 * 2:2], mixed[1:count // 2 * 2:2]
    margin = jnp.minimum(tallies[donor] - 1, limit - tallies[sink]) // 2
    margin = jnp.where((donor == sequence[0]) | (sink == sequence[0]) | (tallies[sink] == 0), 0, jnp.maximum(margin, 0))
    passed = jax.random.randint(jax.random.fold_in(own, 4), (count // 2,), 0, 1 << 20) % (margin + 1)
    tallies = tallies.at[donor].add(-passed).at[sink].add(passed)
    items = jnp.searchsorted(jnp.cumsum(tallies), jnp.arange(rows * top), side="right").astype(jnp.int32)
    table = items.reshape(top, rows).T
    table = table[jax.random.permutation(jax.random.fold_in(own, 1), rows)]
    rotation = jax.random.randint(jax.random.fold_in(own, 2), (rows, 1), 0, top)
    return jnp.take_along_axis(table, (jnp.arange(top)[None, :] + rotation) % top, axis=1)


def load_shares(number_of, total, most, skew, full):
    loads = [(1 << 20) // math.isqrt(rank ** skew) + 1 for rank in range(1, number_of + 1)]
    largest = most if full else min(most, max(-(-total // number_of), total * loads[0] // sum(loads)))
    least = 1 if total - largest >= number_of - 1 else 0
    holding, surplus = [largest] + [least] * (number_of - 1), total - largest - least * (number_of - 1)
    while surplus > 0:
        candidates = [i for i in range(1, number_of) if holding[i] < largest] or [i for i in range(1, number_of) if holding[i] < most]
        mass, remaining = sum([loads[i] for i in candidates]), surplus
        for i in candidates:
            more = min(most - holding[i], max(1, remaining * loads[i] // mass), surplus)
            holding[i] = holding[i] + more
            surplus = surplus - more
    return np.array(holding)


def noise(key, dims, scale, limit, pieces=(), kind=jnp.bfloat16):
    drawn = jax.random.normal(key, dims, jnp.float32) * scale
    if len(pieces) > 0:
        drawn = levels(key, dims, pieces, -0.22, 0.18) * drawn
    return jnp.clip(drawn, min=-limit, max=limit).astype(kind)


def setup_inputs(seed: int = 0) -> dict:
    key_list = jax.random.split(jax.random.key(seed), 12)
    images = noise(key_list[0], (IMAGES, S, D), 1.0, 6.0, ((0, 8),))
    cotangent = noise(key_list[1], (IMAGES, S, D), 1.0, 6.0, ((0, 8),))
    image_count = place_ends(jax.random.randint(key_list[2], (GROUPS,), IMG_DEV - 1, IMG_DEV + 1), jax.random.fold_in(key_list[2], 1), IMG_DEV - 1, IMG_DEV).astype(jnp.int32)
    expert_ids_keys = jax.random.split(jax.random.fold_in(key_list[3], 1), IMAGES * S // TOK_DEV)
    expert_ids_turns = jax.random.permutation(jax.random.fold_in(key_list[3], 3), IMAGES * S // TOK_DEV)
    expert_ids = jax.vmap(lambda own, number: deal_out(jax.random.fold_in(key_list[3], 2), own, number, TOK_DEV, EXPERTS, 2, CAP, 1))(expert_ids_keys, expert_ids_turns).reshape((IMAGES, S, 2))
    ln1_gain = jnp.clip(1.0 + 0.1 * jax.random.normal(key_list[4], (D,), jnp.float32), 0.5, 1.5)
    qkv_weight = noise(key_list[5], (D, 3 * D), D ** -0.5, 0.21875, ((1, 4),))
    proj_weight = noise(key_list[6], (D, D), 0.15, 0.8984375, ((0, 4),))
    ln2_gain = jnp.clip(1.0 + 0.1 * jax.random.normal(key_list[7], (D,), jnp.float32), 0.5, 1.5)
    router_weight = noise(key_list[8], (D, EXPERTS), 0.025, 0.14941406)
    expert_up = noise(key_list[9], (EXPERTS, D, FF), D ** -0.5, 0.21875, ((0, 4), (2, 4)))
    expert_down = noise(key_list[10], (EXPERTS, FF, D), 0.29, 1.6953125, ((0, 4), (1, 4)))
    return dict(images=images, cotangent=cotangent, image_count=image_count, expert_ids=expert_ids, ln1_gain=ln1_gain, qkv_weight=qkv_weight, proj_weight=proj_weight, ln2_gain=ln2_gain, router_weight=router_weight, expert_up=expert_up, expert_down=expert_down)


epsilon = 1e-06
highest = lax.Precision.HIGHEST

@jax.custom_vjp
def low(v):
    return lax.optimization_barrier(v.astype(jnp.bfloat16)).astype(jnp.float32)

@jax.custom_vjp
def low_back(v):
    return v

def low_keep(v):
    return (low(v), None)

def low_pass(kept, grad):
    return (grad,)

def back_keep(v):
    return (v, None)

def back_low(kept, grad):
    return (low(grad),)
low.defvjp(low_keep, low_pass)
low_back.defvjp(back_keep, back_low)

def layer_norm(values, gain_vec):
    center = values - lax.optimization_barrier(jnp.mean(values, axis=-1, keepdims=True))
    spread = lax.optimization_barrier(jnp.mean(center * center, axis=-1, keepdims=True))
    return center * lax.rsqrt(spread + epsilon) * gain_vec

def attend(block_in):
    queries, key_part, value_part = block_in
    scores = low_back(jnp.einsum('bqhd,bkhd->bhqk', queries, key_part, precision=highest) * 0.125)
    probs = jax.nn.softmax(scores, axis=-1)
    return jnp.einsum('bhqk,bkhd->bqhd', low(probs), value_part, precision=highest)

def expert_apply(block_in):
    row_block, up_matrix, down_matrix = block_in
    hidden = low_back(jnp.dot(row_block, up_matrix, precision=highest))
    active = low(jax.nn.gelu(hidden, approximate=False))
    return jnp.dot(active, down_matrix, precision=highest)

def reference(images, cotangent, image_count, expert_ids, ln1_gain, qkv_weight, proj_weight, ln2_gain, router_weight, expert_up, expert_down):
    token_total = IMAGES * S
    id_rows = expert_ids.reshape(GROUPS, TOK_DEV * 2)
    member_int = (id_rows[:, :, None] == jnp.arange(EXPERTS, dtype=jnp.int32)[None, None, :]).astype(jnp.int32)
    slot_index = lax.optimization_barrier(jnp.sum(member_int * jnp.cumsum(member_int, axis=1), axis=2)) - 1
    position = (slot_index + jnp.arange(GROUPS, dtype=jnp.int32)[:, None] * CAP).reshape(-1).astype(jnp.int32)
    flat_ids = expert_ids.reshape(-1).astype(jnp.int32)
    image_index = jnp.arange(IMAGES, dtype=jnp.int32)
    valid = (image_index % IMG_DEV < image_count[image_index // IMG_DEV]).astype(jnp.float32)
    valid_rows = jnp.repeat(valid, S)[:, None]
    pair_ids = expert_ids.reshape(token_total, 2).astype(jnp.int32)

    def forward(inputs, gain_first, qkv_matrix, proj_matrix, gain_second, router_matrix, up_all, down_all):
        flat_in = inputs.reshape(token_total, D)
        normed_first = low(layer_norm(flat_in, gain_first))
        qkv_rows = low(low_back(jnp.dot(normed_first, qkv_matrix, precision=highest)))
        qkv_rows = qkv_rows.reshape(GROUPS, IMG_DEV, S, HEADS, 3, HD)
        attended = lax.map(jax.checkpoint(attend), (qkv_rows[:, :, :, :, 0], qkv_rows[:, :, :, :, 1], qkv_rows[:, :, :, :, 2]))
        attended = low(low_back(attended.reshape(token_total, D)))
        residual = flat_in + low_back(jnp.dot(attended, proj_matrix, precision=highest))
        mixed = low(layer_norm(residual, gain_second))
        gate_probs = jax.nn.softmax(low_back(jnp.dot(mixed, router_matrix, precision=highest)), axis=-1)
        copies = jnp.repeat(mixed, 2, axis=0)
        buffers = jnp.zeros((EXPERTS, GROUPS * CAP, D), jnp.float32).at[flat_ids, position].set(copies)
        outputs = lax.map(jax.checkpoint(expert_apply), (low_back(buffers), up_all, down_all))
        outputs = low(low_back(outputs))
        picked = outputs[flat_ids, position].reshape(token_total, 2, D)
        gate_pick = jnp.take_along_axis(gate_probs, pair_ids, axis=1)
        mixture = lax.optimization_barrier(jnp.sum(gate_pick[:, :, None] * picked, axis=1))
        return (valid_rows * (residual + mixture)).reshape(IMAGES, S, D)
    primal, back_fn = jax.vjp(forward, images.astype(jnp.float32), ln1_gain, qkv_weight.astype(jnp.float32), proj_weight.astype(jnp.float32), ln2_gain, router_weight.astype(jnp.float32), expert_up.astype(jnp.float32), expert_down.astype(jnp.float32))
    grads = back_fn(cotangent.astype(jnp.float32))
    return (primal.astype(jnp.bfloat16), grads[0], grads[1], grads[2], grads[3], grads[4], grads[5], grads[6], grads[7])
```

```python
import jax
import jax.numpy as jnp
from jax import lax
from jax.sharding import PartitionSpec as P

HD = 64
epsilon = 1e-06
BF = jnp.bfloat16
F32 = jnp.float32


def round_up(value, step):
    return -(-value // step) * step


def dot(left, right):
    return jnp.dot(left, right, preferred_element_type=F32)


def dot_nt(left, right):
    return lax.dot_general(left, right, (((1,), (1,)), ((), ())), preferred_element_type=F32)


def dot_tn(left, right):
    return lax.dot_general(left, right, (((0,), (0,)), ((), ())), preferred_element_type=F32)


def normalize(values):
    center = values - jnp.mean(values, axis=-1, keepdims=True)
    scale = lax.rsqrt(jnp.mean(center * center, axis=-1, keepdims=True) + epsilon)
    return center * scale, scale


def normalize_back(normal, scale, dnormal):
    mean_d = jnp.mean(dnormal, axis=-1, keepdims=True)
    mean_dn = jnp.mean(dnormal * normal, axis=-1, keepdims=True)
    return scale * (dnormal - mean_d - normal * mean_dn)


def swap_tensor(block, step):
    size = lax.axis_size("tensor")
    return lax.ppermute(block, "tensor", [(i, i ^ step) for i in range(size)])


def swap_cores(block):
    return lax.ppermute(block, "dp", [(0, 1), (1, 0)])


def swap_by_core(block, first, second):
    size = lax.axis_size("tensor")
    steps = (first, second)
    pairs = [(t * 2 + c, (t ^ steps[c]) * 2 + c) for t in range(size) for c in range(2)]
    return lax.ppermute(block, ("tensor", "dp"), pairs)


def rel_expert(expert):
    size = lax.axis_size("expert")
    if size > 4:
        return expert
    return lax.rem(expert - lax.axis_index("expert") + size, size)


def to_experts(blocks, back=False):
    size = lax.axis_size("expert")
    if size > 4:
        return lax.all_to_all(blocks, "expert", split_axis=0, concat_axis=0, tiled=True)
    rows = blocks.shape[0] // size
    out = [blocks[:rows]]
    for step in range(1, size):
        move = -step if back else step
        pairs = [(i, (i + move) % size) for i in range(size)]
        out.append(lax.ppermute(blocks[step * rows : (step + 1) * rows], "expert", pairs))
    return jnp.concatenate(out, axis=0)


def gather_tensor(block):
    return jnp.concatenate([block] + [swap_tensor(block, s) for s in (1, 2, 3)], axis=0)


def scatter_tensor(blocks):
    rows = blocks.shape[0] // 4
    total = blocks[:rows].astype(F32)
    for step in (1, 2, 3):
        total = total + swap_tensor(blocks[step * rows : (step + 1) * rows], step).astype(F32)
    return total


def gather_weight(shard, axis):
    core = lax.axis_index("dp")
    half = shard.shape[axis] // 2
    mine = lax.dynamic_slice_in_dim(shard, core * half, half, axis)
    other = lax.dynamic_slice_in_dim(shard, (1 - core) * half, half, axis)
    near = swap_by_core(mine, 1, 2)
    pair = jnp.concatenate([mine, near], axis=axis)
    far = swap_by_core(pair, 2, 1)
    rest = jnp.concatenate([near, far], axis=axis)
    return jnp.concatenate([mine, rest, other, swap_cores(rest)], axis=axis)


def scatter_weight_grad(grad, axis):
    half = grad.shape[axis] // 2
    quarter, eighth = half // 2, half // 4
    cut = lambda a, lo, n: lax.slice_in_dim(a, lo, lo + n, axis=axis)
    low = grad.astype(BF)
    summed = cut(grad, 0, half) + 0.0
    arrived = swap_cores(cut(low, half, half)).astype(F32)
    summed = summed + arrived
    sent = cut(summed, quarter, quarter).astype(BF)
    summed = cut(summed, 0, quarter) + swap_by_core(sent, 2, 1).astype(F32)
    sent = cut(summed, eighth, eighth).astype(BF)
    summed = cut(summed, 0, eighth) + swap_by_core(sent, 1, 2).astype(F32)
    peer = swap_cores(summed.astype(BF)).astype(F32)
    core = lax.axis_index("dp")
    first = jnp.where(core == 0, summed, peer)
    second = jnp.where(core == 0, peer, summed)
    return jnp.concatenate([first, second], axis=axis)


def sum_groups(grad):
    size = lax.axis_size("expert")
    if size > 4:
        return lax.psum(grad, ("expert", "dp"))
    core, place = lax.axis_index("dp"), lax.axis_index("expert")
    half = grad.shape[0] // 2
    mine = lax.dynamic_slice_in_dim(grad, core * half, half, 0)
    other = lax.dynamic_slice_in_dim(grad, (1 - core) * half, half, 0)
    mine = mine + swap_cores(other.astype(BF)).astype(F32)
    rows = half // size
    low = mine.astype(BF)
    total = lax.dynamic_slice_in_dim(mine, place * rows, rows, 0)
    for step in range(1, size):
        pairs = [(i, (i + step) % size) for i in range(size)]
        goes = lax.rem(place + step, size)
        block = lax.dynamic_slice_in_dim(low, goes * rows, rows, 0)
        total = total + lax.ppermute(block, "expert", pairs).astype(F32)
    total = total.astype(BF)
    whole = jnp.zeros((half,) + grad.shape[1:], BF)
    whole = lax.dynamic_update_slice_in_dim(whole, total, place * rows, 0)
    for step in range(1, size):
        pairs = [(i, (i + step) % size) for i in range(size)]
        came = lax.rem(place - step + size, size)
        whole = lax.dynamic_update_slice_in_dim(
            whole, lax.ppermute(total, "expert", pairs), came * rows, 0
        )
    peer = swap_cores(whole)
    first = jnp.where(core == 0, whole, peer)
    second = jnp.where(core == 0, peer, whole)
    return jnp.concatenate([first, second], axis=0).astype(F32)


def on_device(
    images,
    cotangent,
    image_count,
    expert_ids,
    ln1_gain,
    qkv_weight,
    proj_weight,
    ln2_gain,
    router_weight,
    expert_up,
    expert_down,
):
    count_img, seq_len, width = images.shape
    tokens = count_img * seq_len
    experts, shares = lax.axis_size("expert"), lax.axis_size("tensor")
    me, my_expert = lax.axis_index("tensor"), lax.axis_index("expert")
    capacity = min(tokens, (2 * tokens // experts // 8 + 2) * 8)
    seq_pad = round_up(seq_len, 16)
    rows_all = count_img * seq_pad
    own = round_up(-(-tokens // shares), 16)
    cap = min(-(-tokens // shares), capacity, (capacity + (shares - 1) * (experts - 1)) // shares)
    cap = round_up(cap, 16)
    heads = qkv_weight.shape[1] // (3 * HD)
    pad = ((0, 0), (0, seq_pad - seq_len), (0, 0))

    up_all = gather_weight(expert_up[0], 1)
    down_all = gather_weight(expert_down[0], 0)

    ids = jnp.pad(expert_ids, pad, constant_values=-1).reshape(rows_all, 2)
    index = lax.iota(jnp.int32, rows_all)
    real = lax.rem(index, seq_pad) < seq_len
    pair = jnp.min(ids, axis=1) * experts + jnp.max(ids, axis=1)
    key = jnp.where(real, pair, experts * experts) * 2048 + index
    rank = jnp.sum((key[None, :] < key[:, None]).astype(jnp.int32), axis=1)
    place = rank // shares
    share = jnp.bitwise_xor(lax.rem(rank, shares), me)
    deal = jnp.where(real, share * own + place, -1)
    perm = (lax.broadcasted_iota(jnp.int32, (shares * own, 1), 0) == deal[None, :]).astype(BF)
    perm_own = perm[:own]
    member = (ids[:, :, None] == lax.iota(jnp.int32, experts)[None, None, :]).astype(F32)
    mine = jnp.where(real & (share == 0), 1.0, 0.0)
    earlier = ((rank[None, :] < rank[:, None]) & (share[None, :] == 0)).astype(BF)
    counts = dot(earlier, jnp.sum(member, axis=1).astype(BF))
    slots = jnp.sum(member * counts[:, None, :], axis=2).astype(jnp.int32)
    row_of = jnp.where((real & (share == 0))[:, None], rel_expert(ids) * cap + slots, -1)
    row_iota = lax.broadcasted_iota(jnp.int32, (experts * cap, 1), 0)
    disp_all = ((row_iota == row_of[None, :, 0]) | (row_iota == row_of[None, :, 1])).astype(BF)
    disp_own = dot_nt(disp_all, perm_own).astype(BF)

    x = jnp.pad(images, pad).reshape(rows_all, width)
    image_of = index // seq_pad
    valid = (real & (image_of < image_count[0])).astype(F32)
    up_low = (jnp.pad(cotangent, pad).reshape(rows_all, width) * valid[:, None].astype(BF))
    rows_up = to_experts(dot(disp_all, up_low).astype(BF))

    normal, _ = normalize(x.astype(F32))
    normed_low = (normal * ln1_gain).astype(BF)
    qkv = dot(normed_low, qkv_weight).astype(BF).reshape(count_img, seq_pad, heads, 3, HD)
    queries, keys, values = qkv[:, :, :, 0], qkv[:, :, :, 1], qkv[:, :, :, 2]
    scores = jnp.einsum("bqhd,bkhd->bhqk", queries, keys, preferred_element_type=F32) * 0.125
    key_real = lax.iota(jnp.int32, seq_pad) < seq_len
    scores = jnp.where(key_real[None, None, None, :], scores, -1e30)
    exps = jnp.exp(scores - jnp.max(scores, axis=-1, keepdims=True))
    probs = exps / jnp.sum(exps, axis=-1, keepdims=True)
    probs_low = probs.astype(BF)
    attended = jnp.einsum("bhqk,bkhd->bqhd", probs_low, values, preferred_element_type=F32)
    attended = attended.astype(BF).reshape(rows_all, heads * HD)
    att_perm = dot(perm, attended).astype(BF)
    partial = dot(att_perm, proj_weight).astype(BF)
    attn = scatter_tensor(partial)

    x_own = dot(perm_own, x)
    residual = x_own + attn
    normal2, scale2 = normalize(residual)
    mixed = (normal2 * ln2_gain).astype(BF)
    rows_in = to_experts(dot(disp_own, mixed).astype(BF))

    gate_probs = jax.nn.softmax(dot(rows_in, router_weight), axis=-1)
    onehot = (lax.iota(jnp.int32, experts) == my_expert).astype(F32)[None, :]
    gate = jnp.sum(gate_probs * onehot, axis=1, keepdims=True)
    hidden = dot(rows_in, up_all)
    cdf = 0.5 * (1.0 + lax.erf(hidden * (0.5**0.5)))
    active = (hidden * cdf).astype(BF)
    slope = cdf + hidden * jnp.exp(-0.5 * hidden * hidden) * 0.3989422804014327
    out_rows = dot(active, down_all).astype(BF).astype(F32)
    upstream_rows = rows_up.astype(F32)
    dgate = jnp.sum(upstream_rows * out_rows, axis=1, keepdims=True)
    dout = (gate * upstream_rows).astype(BF)
    dhidden = (dot_nt(dout, down_all) * slope).astype(BF)
    dlogits = (gate_probs * dgate * (onehot - gate)).astype(BF)
    dmixed_rows = dot_nt(dhidden, up_all) + dot_nt(dlogits, router_weight)
    back_mixed = to_experts(dmixed_rows.astype(BF), True)
    back_out = to_experts((gate * out_rows).astype(BF), True)
    grad_router = dot_tn(rows_in, dlogits)
    grad_down = scatter_weight_grad(dot_tn(active, dout), 0)
    grad_up = scatter_weight_grad(dot_tn(rows_in, dhidden), 1)

    up_own = dot(perm_own, up_low)
    dmixed = dot_tn(disp_own, back_mixed)
    grad_ln2 = jnp.sum(dmixed * normal2, axis=0)
    dresidual = up_own + normalize_back(normal2, scale2, dmixed * ln2_gain)
    dattn = gather_tensor(dresidual.astype(BF))
    mixture = dot_tn(disp_own, back_out)
    out_own = (residual + mixture).astype(BF)
    block_output = dot_tn(perm, gather_tensor(out_own)) * valid[:, None]
    block_output = block_output.astype(BF).reshape(count_img, seq_pad, width)[:, :seq_len]

    grad_proj = dot_tn(att_perm, dattn)
    dattended = dot_nt(dattn, proj_weight).astype(BF)
    dattended = dot_tn(perm, dattended).astype(BF).reshape(count_img, seq_pad, heads, HD)
    dprobs = jnp.einsum("bqhd,bkhd->bhqk", dattended, values, preferred_element_type=F32)
    dscores = probs * (dprobs - jnp.sum(probs * dprobs, axis=-1, keepdims=True))
    dscores = dscores.astype(BF)
    dq = jnp.einsum("bhqk,bkhd->bqhd", dscores, keys, preferred_element_type=F32) * 0.125
    dk = jnp.einsum("bhqk,bqhd->bkhd", dscores, queries, preferred_element_type=F32) * 0.125
    dv = jnp.einsum("bhqk,bqhd->bkhd", probs_low, dattended, preferred_element_type=F32)
    dqkv = jnp.stack([dq, dk, dv], axis=3).astype(BF).reshape(rows_all, heads * 3 * HD)
    dnormed = dot_nt(dqkv, qkv_weight)
    grad_ln1 = jnp.sum(dnormed * normal, axis=0)
    dn_own = scatter_tensor(dot(perm, dnormed.astype(BF)).astype(BF))
    grad_qkv = dot_tn(normed_low, dqkv)
    small = lax.psum((grad_ln1, grad_ln2, grad_router), ("expert", "dp", "tensor"))
    dense = sum_groups(
        jnp.concatenate([grad_qkv, grad_proj.reshape(-1, grad_qkv.shape[1])], axis=0)
    )
    normal_own, scale_own = normalize(x_own)
    input_own = dresidual + normalize_back(normal_own, scale_own, dn_own * ln1_gain)
    input_grad = dot_tn(perm, gather_tensor(input_own.astype(BF)))
    input_grad = input_grad.reshape(count_img, seq_pad, width)[:, :seq_len]
    return (
        block_output,
        input_grad,
        small[0],
        dense[:width],
        dense[width:].reshape(proj_weight.shape),
        small[1],
        small[2],
        grad_up[None],
        grad_down[None],
    )


def solution(mesh):
    placed = (
        P(("expert", "dp"), None, None),
        P(("expert", "dp"), None, None),
        P(("expert", "dp")),
        P(("expert", "dp"), None, None),
        P(),
        P(None, "tensor"),
        P("tensor", None),
        P(),
        P(),
        P("expert", None, "tensor"),
        P("expert", "tensor", None),
    )
    return jax.shard_map(
        on_device,
        mesh=mesh,
        in_specs=placed,
        out_specs=(
            P(("expert", "dp"), None, None),
            P(("expert", "dp"), None, None),
            P(),
            P(None, "tensor"),
            P("tensor", None),
            P(),
            P(),
            P("expert", None, "tensor"),
            P("expert", "tensor", None),
        ),
        check_vma=False,
    )
```

```python
import functools

import jax
import jax.numpy as jnp
from jax import lax
from jax.experimental import pallas as pl
from jax.experimental.pallas import tpu as pltpu
from jax.sharding import PartitionSpec as P

HD = 64
LANES = 128
LONG = 1 << 36
SPILLS = 10 << 20
epsilon = 1e-06
BF = jnp.bfloat16
F32 = jnp.float32


def round_up(value, step):
    return -(-value // step) * step


def dot(left, right):
    return jnp.dot(left, right, preferred_element_type=F32)


def dot_nt(left, right):
    return lax.dot_general(left, right, (((1,), (1,)), ((), ())), preferred_element_type=F32)


def dot_tn(left, right):
    return lax.dot_general(left, right, (((0,), (0,)), ((), ())), preferred_element_type=F32)


def normalize(values):
    center = values - jnp.mean(values, axis=-1, keepdims=True)
    scale = lax.rsqrt(jnp.mean(center * center, axis=-1, keepdims=True) + epsilon)
    return center * scale, scale


def normalize_back(normal, scale, dnormal):
    mean_d = jnp.mean(dnormal, axis=-1, keepdims=True)
    mean_dn = jnp.mean(dnormal * normal, axis=-1, keepdims=True)
    return scale * (dnormal - mean_d - normal * mean_dn)


def after(value, *others):
    return lax.optimization_barrier((value,) + others)[0]


def local(kernel, outs, *args, scratch=(), smem=(), long=False):
    shapes = [jax.ShapeDtypeStruct(shape, dtype) for shape, dtype in outs]
    place = lambda i: pltpu.SMEM if i in smem else pltpu.VMEM
    held = [*args, *shapes, *(jax.ShapeDtypeStruct(shape, dtype) for shape, dtype in scratch)]
    size = sum(a.size * a.dtype.itemsize for a in held)
    return pl.pallas_call(
        kernel,
        out_shape=shapes,
        in_specs=[pl.BlockSpec(memory_space=place(i)) for i in range(len(args))],
        out_specs=[pl.BlockSpec(memory_space=pltpu.VMEM)] * len(outs),
        scratch_shapes=[pltpu.VMEM(shape, dtype) for shape, dtype in scratch],
        compiler_params=pltpu.CompilerParams(vmem_limit_bytes=min(size + SPILLS, 60 << 20)),
        cost_estimate=pl.CostEstimate(
            flops=LONG if long else 0, bytes_accessed=0, transcendentals=0
        ),
    )(*args)


def spread(rows, columns, step):
    row = lax.broadcasted_iota(jnp.int32, (rows, columns), 0)
    column = lax.broadcasted_iota(jnp.int32, (rows, columns), 1)
    if step:
        row, column = column, row
    same = (row >> 6 == column >> 7) & ((row & 63) == (column & 127))
    return same.astype(F32).astype(BF)


def pack_kernel(core_ref, up_ref, down_ref, mine_ref, other_ref):
    width, half = up_ref.shape[0], up_ref.shape[1] // 2
    down_t = down_ref[...].T
    first = core_ref[0] == 0

    @pl.when(first)
    def _():
        mine_ref[:width] = up_ref[:, :half]
        mine_ref[width:] = down_t[:, :half]
        other_ref[:width] = up_ref[:, half:]
        other_ref[width:] = down_t[:, half:]

    @pl.when(jnp.logical_not(first))
    def _():
        mine_ref[:width] = up_ref[:, half:]
        mine_ref[width:] = down_t[:, half:]
        other_ref[:width] = up_ref[:, :half]
        other_ref[width:] = down_t[:, :half]


def put_blocks(refs, value):
    rows = refs[0].shape[0]
    for s, ref in enumerate(refs):
        ref[...] = value[s * rows : (s + 1) * rows]


def put_parts(refs, value):
    rows = refs[0].shape[0]
    refs[0][...] = value[:rows]
    refs[1][...] = value[rows : 2 * rows]
    refs[2][...] = value[2 * rows :]


def route_kernel(seq_len, count_ref, deal_row, rows_ref, cot_ref, perm, up_own, disp_all, *refs):
    ups, held = refs[:-1], refs[-1]
    seq_pad = held.shape[0] // cot_ref.shape[0]
    own = up_own.shape[0]
    hit = lax.broadcasted_iota(jnp.int32, perm.shape, 0) == deal_row[...]
    perm[...] = hit.astype(F32).astype(BF)
    held[...] = jnp.zeros_like(held)
    for image in range(cot_ref.shape[0]):
        keep = (count_ref[0] > image).astype(F32)
        at = image * seq_pad
        held[at : at + seq_len] = cot_ref[image].astype(F32) * keep
    place = lax.broadcasted_iota(jnp.int32, disp_all.shape, 0)
    hit = (place == rows_ref[0:1]) | (place == rows_ref[1:2])
    disp = hit.astype(F32).astype(BF)
    disp_all[...] = disp
    upstream = held[...].astype(BF)
    put_blocks(ups, dot(disp, upstream).astype(BF))
    up_own[...] = dot(perm[:own], upstream).astype(BF)


def qkv_kernel(seq_len, x_ref, gain, weight_t, normed, wide_t, qkv, x_pad, held):
    seq_pad = held.shape[0] // x_ref.shape[0]
    held[...] = jnp.zeros_like(held)
    for image in range(x_ref.shape[0]):
        held[image * seq_pad : image * seq_pad + seq_len] = x_ref[image].astype(F32)
    values = held[...]
    x_pad[...] = values.astype(BF)
    normal, _ = normalize(values)
    low = (normal * gain[...]).astype(BF)
    normed[...] = low
    wide_low = dot(spread(wide_t.shape[0], weight_t.shape[0], True), weight_t[...]).astype(BF)
    wide_t[...] = wide_low
    qkv[...] = dot_nt(low, wide_low).astype(BF)


def pieces(qkv, rows, head):
    at = lambda c: qkv[rows, (head * 3 + c) * LANES : (head * 3 + c + 1) * LANES]
    return at(0), at(1), at(2)


def softmax_of(queries, keys, seq_len):
    scores = dot_nt(queries, keys) * 0.125
    real = lax.broadcasted_iota(jnp.int32, scores.shape, 1) < seq_len
    scores = jnp.where(real, scores, -1e30)
    exps = jnp.exp(scores - jnp.max(scores, axis=-1, keepdims=True))
    return exps / jnp.sum(exps, axis=-1, keepdims=True)


def attend_kernel(seq_len, count_img, qkv, perm, proj, att, *refs):
    parts, held = refs[:-1], refs[-1]
    heads = qkv.shape[1] // (3 * LANES)
    seq_pad = qkv.shape[0] // count_img
    for image in range(count_img):
        rows = slice(image * seq_pad, (image + 1) * seq_pad)
        for head in range(heads):
            queries, keys, values = pieces(qkv, rows, head)
            probs = softmax_of(queries, keys, seq_len).astype(BF)
            held[rows, head * LANES : (head + 1) * LANES] = dot(probs, values).astype(BF)
    att_perm = dot(perm[...], held[...]).astype(BF)
    att[...] = att_perm
    wide = dot(spread(held.shape[1], proj.shape[0], True), proj[...]).astype(BF)
    put_parts(parts, dot(att_perm, wide).astype(BF))


def mix_kernel(part, first, second, x_pad, perm, gain, disp_all, residual, x_own, disp, *outs):
    own = part.shape[0]
    perm_own = perm[:own]
    own_x = dot(perm_own, x_pad[...])
    x_own[...] = own_x.astype(BF)
    own_disp = dot_nt(disp_all[...], perm_own).astype(BF)
    disp[...] = own_disp
    attn = part[...].astype(F32) + first[:own].astype(F32)
    whole = own_x + (attn + second[...].astype(F32))
    residual[...] = whole
    normal, _ = normalize(whole)
    put_blocks(outs, dot(own_disp, (normal * gain[...]).astype(BF)).astype(BF))


def gelu_parts(hidden):
    size = jnp.abs(hidden)
    density = jnp.exp(-0.5 * (hidden * hidden))
    t = 1.0 / (1.0 + (0.3275911 * 0.5**0.5) * size)
    poly = 0.5 * 1.061405429 * t - 0.5 * 1.453152027
    poly = poly * t + 0.5 * 1.421413741
    poly = poly * t - 0.5 * 0.284496736
    poly = poly * t + 0.5 * 0.254829592
    tail = poly * t * density
    cdf = jnp.where(hidden < 0.0, tail, 1.0 - tail)
    return cdf, cdf + hidden * density * 0.3989422804014327


def expert_kernel(blocks, packs, last, *refs):
    refs = list(refs)
    take = lambda n: [refs.pop(0) for _ in range(n)]
    rows_refs, up_refs, pack_refs = take(blocks), take(blocks), take(packs)
    router, mark = take(2)
    earlier = take(2) if last else None
    rows = jnp.concatenate([r[...] for r in rows_refs], axis=0)
    upstream = jnp.concatenate([r[...] for r in up_refs], axis=0).astype(F32)
    experts = mark.shape[0]
    logits = dot_nt(rows, router[...])
    lane = lax.broadcasted_iota(jnp.int32, logits.shape, 1)
    logits = jnp.where(lane < experts, logits, -1e30)
    exps = jnp.exp(logits - jnp.max(logits, axis=-1, keepdims=True))
    gates = exps / jnp.sum(exps, axis=-1, keepdims=True)
    onehot = mark[0:1]
    gate = jnp.sum(gates * onehot, axis=1, keepdims=True)
    dout = (gate * upstream).astype(BF)
    if last:
        backs = take(blocks)
        active, dhidden, dlog_t, acc, dacc = refs
        acc[...], dacc[...] = earlier[0][...], earlier[1][...]
    else:
        acc, dacc, active, dhidden, dout_ref = refs
        dout_ref[...] = dout
    for p, pack in enumerate(pack_refs):
        half, width = pack.shape[1], pack.shape[0] // 2
        up, down_t = pack[:width], pack[width:]
        hidden = dot(rows, up)
        cdf, slope = gelu_parts(hidden)
        low = (hidden * cdf).astype(BF)
        active[:, p * half : (p + 1) * half] = low
        dlow = (dot(dout, down_t) * slope).astype(BF)
        dhidden[:, p * half : (p + 1) * half] = dlow
        if p == 0 and not last:
            acc[...] = dot_nt(low, down_t)
            dacc[...] = dot_nt(dlow, up)
        else:
            acc[...] += dot_nt(low, down_t)
            dacc[...] += dot_nt(dlow, up)
    if last:
        out_rows = acc[...].astype(BF).astype(F32)
        mixture = (gate * out_rows).astype(BF)
        dgate = jnp.sum(upstream * out_rows, axis=1, keepdims=True)
        dlog = (gates * dgate * (onehot - gate)).astype(BF)
        back = (dacc[...] + dot(dlog, router[...])).astype(BF)
        put_blocks(backs, jnp.concatenate([back, mixture], axis=1))
        dlog_t[...] = dot_tn(dlog, rows)


def weight_kernel(blocks, columns, *refs):
    refs = list(refs)
    rows = jnp.concatenate([refs.pop(0)[...] for _ in range(blocks)], axis=0)
    *arrays, dout, keep, sent = refs
    half, width = keep.shape[2], rows.shape[1]
    rows_t, dout_t = rows.T, dout[...].T
    for i, (call, place) in enumerate(columns):
        target = (sent, keep)[i // 2]
        active, dhidden = arrays[2 * call], arrays[2 * call + 1]
        at = slice(place * half, (place + 1) * half)
        target[i % 2, :width] = dot(rows_t, dhidden[:, at]).astype(BF)
        target[i % 2, width:] = dot(dout_t, active[:, at]).astype(BF)


def add_kernel(*refs):
    total = refs[0][...].astype(F32)
    for ref in refs[1:-1]:
        total = total + ref[...].astype(F32)
    refs[-1][...] = total.astype(refs[-1].dtype)


def add_split_kernel(*refs):
    total = refs[0][...].astype(F32)
    for ref in refs[1:-2]:
        total = total + ref[...].astype(F32)
    refs[-2][...] = total[0].astype(BF)
    refs[-1][...] = total[1].astype(BF)


def combine_kernel(blocks, used, experts, *refs):
    refs = list(refs)
    back = jnp.concatenate([refs.pop(0)[...] for _ in range(blocks)], axis=0)
    disp, residual, up_own, gain, dlog_t, dresidual, dattn, out_own = refs
    both = dot_tn(disp[...], back)
    dmixed, mixture = both[:, : dattn.shape[1]], both[:, dattn.shape[1] :]
    out_own[...] = (residual[...] + mixture).astype(BF)
    normal, scale = normalize(residual[...])
    grad_ln2 = jnp.sum(dmixed * normal, axis=0, keepdims=True)
    total = up_own[...].astype(F32) + normalize_back(normal, scale, dmixed * gain[...])
    dresidual[...] = total
    row = lax.broadcasted_iota(jnp.int32, (total.shape[0], 1), 0)
    total = jnp.where(row < used, total, 0.0)
    total = total + jnp.where(row == used, grad_ln2, 0.0)
    for e in range(experts):
        total = total + jnp.where(row == used + 1 + e, dlog_t[e : e + 1], 0.0)
    dattn[...] = total.astype(BF)


def attend_back_kernel(seq_len, count_img, used, *refs):
    pair, far, qkv, x_ref, perm, proj, wide_t, dqkv, *dns, held = refs
    dattn = jnp.concatenate([pair[...], far[...]], axis=0)
    heads = qkv.shape[1] // (3 * LANES)
    seq_pad = qkv.shape[0] // count_img
    wide_proj = dot(spread(heads * LANES, proj.shape[0], True), proj[...]).astype(BF)
    datt = dot_nt(dattn, wide_proj).astype(BF)
    held[...] = dot_tn(perm[...], datt).astype(BF)
    for image in range(count_img):
        rows = slice(image * seq_pad, (image + 1) * seq_pad)
        for head in range(heads):
            queries, keys, values = pieces(qkv, rows, head)
            probs = softmax_of(queries, keys, seq_len)
            d_out = held[rows, head * LANES : (head + 1) * LANES]
            dprobs = dot_nt(d_out, values)
            dscores = probs * (dprobs - jnp.sum(probs * dprobs, axis=-1, keepdims=True))
            dscores = dscores.astype(BF)
            at = head * 3 * LANES
            dqkv[rows, at : at + LANES] = (dot(dscores, keys) * 0.125).astype(BF)
            dqkv[rows, at + LANES : at + 2 * LANES] = (dot_tn(dscores, queries) * 0.125).astype(BF)
            dqkv[rows, at + 2 * LANES : at + 3 * LANES] = dot_tn(probs.astype(BF), d_out).astype(BF)
    dnormed = dot(dqkv[...], wide_t[...])
    normal, _ = normalize(x_ref[...].astype(F32))
    grad_ln1 = jnp.sum(dnormed * normal, axis=0, keepdims=True)
    own = pair.shape[0] // 2
    out = dot(perm[...], dnormed.astype(BF))
    row = lax.broadcasted_iota(jnp.int32, (out.shape[0], 1), 0)
    carries = row == used
    for s in range(1, out.shape[0] // own):
        carries = carries | (row == used + s * own)
    put_parts(dns, (out + jnp.where(carries, grad_ln1, 0.0)).astype(BF))


def dense_kernel(core_ref, pair, far, att, normed, dqkv, mine, *refs):
    others, held = refs[:-1], refs[-1]
    dattn = jnp.concatenate([pair[...], far[...]], axis=0)
    qkv_wide = dot_tn(normed[...], dqkv[...]).astype(BF)
    columns = qkv_wide.shape[1] // 2
    held[:, :columns] = dot(qkv_wide, spread(2 * columns, columns, True))
    proj_wide = dot_tn(dattn, att[...]).astype(BF)
    rows = proj_wide.shape[1] // 2
    held[:, columns:] = dot(proj_wide, spread(2 * rows, rows, True))
    half = mine.shape[0]
    core = core_ref[0]
    mine[...] = held[pl.ds(pl.multiple_of(core * half, half), half)].astype(BF)
    put_blocks(others, held[pl.ds(pl.multiple_of((1 - core) * half, half), half)].astype(BF))


def dense_split_kernel(place_ref, mine, low, high, *refs):
    outs, held = refs[:-1], refs[-1]
    arrived = jnp.concatenate([low[...], high[...]], axis=0)
    held[...] = mine[...].astype(F32) + arrived.astype(F32)
    rows = outs[0].shape[0]
    for s, out in enumerate(outs):
        at = lax.rem(place_ref[0] + s, len(outs)) * rows
        out[...] = held[pl.ds(pl.multiple_of(at, rows), rows)].astype(BF)


def dense_sum_kernel(late, *refs):
    out = refs[-1]
    total = refs[0][...].astype(F32)
    for ref in refs[1:-1]:
        total = total + ref[...].astype(F32)
    rows = total.shape[0]
    out[:rows] = total.astype(BF)
    out[rows:] = late[...].astype(BF)


def dense_join_kernel(place_ref, *refs):
    out, blocks = refs[-1], refs[:-1]
    rows = (out.shape[0] - blocks[0].shape[0]) // (len(blocks) - 1)
    late = jnp.zeros((blocks[0].shape[0] - rows, out.shape[1]), F32)
    for s, block in enumerate(blocks):
        at = lax.rem(place_ref[0] - s + len(blocks), len(blocks)) * rows
        out[pl.ds(pl.multiple_of(at, rows), rows)] = block[:rows]
        late = late + block[rows:].astype(F32)
    out[rows * len(blocks) :] = late.astype(BF)


def dense_out_kernel(core_ref, mine, peer, qkv, proj, late):
    half = qkv.shape[1] // 2
    core = core_ref[0]
    columns = qkv.shape[0]
    late[...] = mine[half:].astype(F32) + peer[half:].astype(F32)

    def put(block, at):
        turned = block[:half].astype(F32).T
        qkv[:, at : at + half] = turned[:columns]
        proj[:, at : at + half] = turned[columns:]

    @pl.when(core == 0)
    def _():
        put(mine[...], 0)
        put(peer[...], half)

    @pl.when(core != 0)
    def _():
        put(peer[...], 0)
        put(mine[...], half)


def add_rows_kernel(mine, arrived, out):
    rows = out.shape[0]
    out[...] = (mine[...].astype(F32) + arrived[rows:].astype(F32)).astype(BF)


def input_kernel(used, spare, dn, first, second, x_own, dresidual, gain, pair, far, out, late):
    own = x_own.shape[0]
    total = dn[...].astype(F32) + first[:own].astype(F32) + second[...].astype(F32)
    normal, scale = normalize(x_own[...].astype(F32))
    back = dresidual[...] + normalize_back(normal, scale, total * gain[...])
    out[...] = back.astype(BF)
    late[...] = jnp.zeros_like(late)
    late[0:1] = total[used : used + 1]
    small = [ref[s * own + used : s * own + used + spare] for ref in (pair, far) for s in range(2)]
    late[1 : 1 + spare] = sum(block.astype(F32) for block in small)


def place_kernel(seq_len, count_ref, pair, far, perm, out):
    low = jnp.concatenate([pair[...], far[...]], axis=0)
    rows = dot_tn(perm[...], low)
    seq_pad = rows.shape[0] // out.shape[0]
    for image in range(out.shape[0]):
        keep = (count_ref[0] > image).astype(F32)
        block = rows[image * seq_pad : image * seq_pad + seq_len] * keep
        out[image] = block.astype(out.dtype)


def weight_out_kernel(core_ref, mine_ref, arrived_ref, peer_ref, up, down):
    width, half = mine_ref.shape[0] // 2, mine_ref.shape[1]
    mine = mine_ref[...].astype(F32) + arrived_ref[...].astype(F32)
    peer = peer_ref[...].astype(F32)

    def put(block, at):
        up[0, :, at : at + half] = block[:width]
        down[0, at : at + half] = block[width:].T

    @pl.when(core_ref[0] == 0)
    def _():
        put(mine, 0)
        put(peer, half)

    @pl.when(core_ref[0] != 0)
    def _():
        put(peer, 0)
        put(mine, half)


def swap_tensor(block, step):
    size = lax.axis_size("tensor")
    return lax.ppermute(block, "tensor", [(i, i ^ step) for i in range(size)])


def swap_cores(block):
    return lax.ppermute(block, "dp", [(0, 1), (1, 0)])


def swap_by_core(block, first, second):
    size = lax.axis_size("tensor")
    steps = (first, second)
    pairs = [(t * 2 + c, (t ^ steps[c]) * 2 + c) for t in range(size) for c in range(2)]
    return lax.ppermute(block, ("tensor", "dp"), pairs)


def rel_expert(expert):
    size = lax.axis_size("expert")
    if size > 4:
        return expert
    return lax.rem(expert - lax.axis_index("expert") + size, size)


def send_expert(blocks):
    size = lax.axis_size("expert")
    steps = range(1, size)
    return [
        lax.ppermute(blocks[s], "expert", [(i, (i + s) % size) for i in range(size)]) for s in steps
    ]


def to_experts(blocks, back=False):
    size = lax.axis_size("expert")
    if len(blocks) == 1:
        return [lax.all_to_all(blocks[0], "expert", split_axis=0, concat_axis=0, tiled=True)]
    out = [blocks[0]]
    for step in range(1, size):
        move = -step if back else step
        pairs = [(i, (i + move) % size) for i in range(size)]
        out.append(lax.ppermute(blocks[step], "expert", pairs))
    return out


def gather_start(block):
    return jnp.concatenate([block, swap_by_core(block, 2, 1)], axis=0)


def gather_end(pair):
    return swap_by_core(pair, 1, 2)


def scatter_end(kept, first):
    (sent,) = local(add_rows_kernel, [(kept.shape, BF)], kept, first)
    return swap_by_core(sent, 2, 1), sent


def sum_groups(mine, others, late_of, meanwhile):
    size = lax.axis_size("expert")
    half, width = mine.shape
    if size > 4:
        late = late_of([mine])
        meanwhile()
        arrived = jnp.concatenate([swap_cores(other) for other in others], axis=0)
        mine = mine + arrived.astype(F32)
        mine, late = lax.psum((mine, late), "expert")
        block = jnp.concatenate([mine, late], axis=0).astype(BF)
        return block, swap_cores(block)
    place = lax.axis_index("expert")[None]
    rows = half // size
    arrived = [swap_cores(other) for other in others]
    blocks = local(
        dense_split_kernel,
        [((rows, width), BF)] * size,
        place,
        mine,
        *arrived,
        scratch=[((half, width), F32)],
        smem=(0,),
    )
    came = send_expert(blocks)
    late = late_of(came)
    extra = late.shape[0]
    (total,) = local(dense_sum_kernel, [((rows + extra, width), BF)], late, blocks[0], *came)
    came = send_expert([total] * size)
    (block,) = local(
        dense_join_kernel,
        [((half + extra, width), BF)],
        place,
        after(total, *meanwhile()),
        *came,
        smem=(0,),
    )
    return block, swap_cores(block)


def on_device(
    images,
    cotangent,
    image_count,
    expert_ids,
    ln1_gain,
    qkv_weight,
    proj_weight,
    ln2_gain,
    router_weight,
    expert_up,
    expert_down,
):
    count_img, seq_len, width = images.shape
    tokens = count_img * seq_len
    experts, shares = lax.axis_size("expert"), lax.axis_size("tensor")
    me, my_expert = lax.axis_index("tensor"), lax.axis_index("expert")
    capacity = min(tokens, (2 * tokens // experts // 8 + 2) * 8)
    seq_pad = round_up(seq_len, 16)
    rows_all = count_img * seq_pad
    used = -(-tokens // shares)
    spare = experts + 1
    own = round_up(used + spare, 16)
    cap = min(used, capacity, (capacity + (shares - 1) * (experts - 1)) // shares)
    cap = round_up(cap, 16)
    slots_all = experts * cap
    half = expert_up.shape[2] // 2
    wide = 2 * qkv_weight.shape[1]
    att_width = 2 * proj_weight.shape[0]
    pad = ((0, 0), (0, seq_pad - seq_len), (0, 0))
    core = lax.axis_index("dp")[None]
    gain1, gain2 = ln1_gain[None], ln2_gain[None]

    pack = ((2 * width, half), BF)
    mine, other = local(
        pack_kernel, [pack] * 2, core, expert_up[0], expert_down[0], smem=(0,)
    )
    near = swap_by_core(mine, 1, 2)

    ids = jnp.pad(expert_ids, pad, constant_values=-1).reshape(rows_all, 2)
    index = lax.iota(jnp.int32, rows_all)
    real = lax.rem(index, seq_pad) < seq_len
    pair = jnp.min(ids, axis=1) * experts + jnp.max(ids, axis=1)
    key = jnp.where(real, pair, experts * experts) * 2048 + index
    rank = jnp.sum((key[None, :] < key[:, None]).astype(jnp.int32), axis=1)
    share = jnp.bitwise_xor(lax.rem(rank, shares), me)
    turned = (share & 1) * 2 + (share >> 1)
    share = jnp.where(lax.axis_index("dp") == 0, turned, share)
    deal = jnp.where(real, share * own + rank // shares, -1)
    member = (ids[:, :, None] == lax.iota(jnp.int32, experts)[None, None, :]).astype(F32)
    earlier = ((rank[None, :] < rank[:, None]) & (share[None, :] == 0)).astype(BF)
    counts = dot(earlier, jnp.sum(member, axis=1).astype(BF))
    slots = jnp.sum(member * counts[:, None, :], axis=2).astype(jnp.int32)
    row_of = jnp.where((real & (share == 0))[:, None], rel_expert(ids) * cap + slots, -1)
    parts = 1 if experts > 4 else experts
    block = ((slots_all // parts, width), BF)
    perm, up_own, disp_all, *rows_up = local(
        functools.partial(route_kernel, seq_len),
        [
            ((shares * own, rows_all), BF),
            ((own, width), BF),
            ((slots_all, rows_all), BF),
            *[block] * parts,
        ],
        image_count,
        deal[None],
        row_of.T,
        after(cotangent, mine),
        scratch=[((rows_all, width), F32)],
        smem=(0,),
    )
    rows_up = to_experts(rows_up)

    normed, wide_t, qkv, x = local(
        functools.partial(qkv_kernel, seq_len),
        [((rows_all, width), BF), ((wide, width), BF), ((rows_all, wide), BF), ((rows_all, width), BF)],
        after(images, perm),
        gain1,
        qkv_weight.T,
        scratch=[((rows_all, width), F32)],
    )
    near = after(near, qkv)
    far = [swap_by_core(after(mine, near), 2, 1)]
    rest = [swap_cores(near)]
    share_block = ((own, width), BF)
    share_parts = [share_block, share_block, ((2 * own, width), BF)]
    att, *part = local(
        functools.partial(attend_kernel, seq_len, count_img),
        [((shares * own, att_width), BF), *share_parts],
        qkv,
        perm,
        proj_weight,
        scratch=[((rows_all, att_width), BF)],
    )
    first = swap_by_core(after(part[2], *rows_up), 1, 2)
    rest.append(swap_cores(after(far[0], first)))
    second, sent = scatter_end(after(part[1], far[0]), first)
    far.append(swap_by_core(after(near, first), 2, 1))

    residual, x_own, disp, *sent = local(
        mix_kernel,
        [((own, width), F32), share_block, ((slots_all, own), BF), *[block] * parts],
        part[0],
        after(first, *rest),
        second,
        x,
        perm,
        gain2,
        disp_all,
        long=True,
    )
    rows_in = to_experts(sent)
    rest.append(swap_cores(after(far[1], sent[0])))

    mark = jnp.zeros((experts, LANES), F32).at[:, my_expert].set(1.0)
    router = jnp.pad(router_weight.T, ((0, LANES - experts), (0, 0)))
    packs = [mine, near, far[0], other, *rest[:2]]
    low, full = ((slots_all, width), BF), ((slots_all, width), F32)
    many = lambda packs: ((slots_all, len(packs) * half), BF)
    acc, dacc, active, dhidden, dout = local(
        functools.partial(expert_kernel, parts, len(packs), False),
        [full, full, many(packs), many(packs), low],
        *rows_in,
        *rows_up,
        *packs,
        router,
        mark,
        long=True,
    )
    packs = [far[1], rest[2]]
    results = local(
        functools.partial(expert_kernel, parts, len(packs), True),
        [*[((slots_all // parts, 2 * width), BF)] * parts, many(packs), many(packs), ((LANES, width), F32)],
        *rows_in,
        *rows_up,
        *packs,
        router,
        mark,
        acc,
        dacc,
        scratch=[full, full],
    )
    back = list(results[:parts])
    active_last, dhidden_last, dlog_t = results[parts:]
    back = to_experts(back, True)
    two = ((2,) + pack[0], BF)
    grads = lambda columns, dout: local(
        functools.partial(weight_kernel, parts, columns),
        [two] * 2,
        *rows_in,
        active,
        dhidden,
        active_last,
        dhidden_last,
        dout,
    )
    keep_b, sent_b = grads(((0, 5), (1, 1), (0, 2), (1, 0)), dout)
    came_b = swap_cores(sent_b)
    keep_a, sent_a = grads(((0, 3), (0, 4), (0, 0), (0, 1)), after(dout, sent_b))
    came_a = swap_cores(sent_a)

    dresidual, dattn, out_own = local(
        functools.partial(combine_kernel, len(back), used, experts),
        [((own, width), F32), share_block, share_block],
        after(back[0], sent_a),
        *back[1:],
        disp,
        residual,
        up_own,
        gain2,
        dlog_t,
        long=True,
    )
    dattn_pair = gather_start(dattn)
    dattn_far = gather_end(dattn_pair)
    (sum_b,) = local(add_kernel, [two], keep_b, after(came_b, came_a, dattn))
    came_far = swap_by_core(sum_b, 2, 1)
    out_pair = gather_start(after(out_own, dattn_pair, sum_b))
    out_far = gather_end(out_pair)

    dqkv, *dn = local(
        functools.partial(attend_back_kernel, seq_len, count_img, used),
        [(qkv.shape, BF), *share_parts],
        dattn_pair,
        dattn_far,
        after(qkv, sum_b, out_pair),
        x,
        perm,
        proj_weight,
        wide_t,
        scratch=[((rows_all, att_width), BF)],
        long=True,
    )
    first = swap_by_core(dn[2], 1, 2)
    second, sent = scatter_end(after(dn[1], came_far, out_far), first)
    dense, *other = local(
        dense_kernel,
        [((width // 2, width), BF), *[((width // 4, width), BF)] * 2],
        core,
        dattn_pair,
        after(dattn_far, dn[2]),
        att,
        normed,
        dqkv,
        scratch=[((width, width), F32)],
        smem=(0,),
    )
    grad, grad_sent = local(add_split_kernel, [pack] * 2, keep_a, came_a, after(came_far, sent))
    came_near = swap_by_core(grad_sent, 1, 2)
    input_in = []

    def input_of(sent):
        own_block, late = local(
            functools.partial(input_kernel, used, spare),
            [share_block, ((round_up(spare + 1, 16), width), F32)],
            after(dn[0], grad, *sent),
            first,
            second,
            x_own,
            dresidual,
            gain1,
            dattn_pair,
            dattn_far,
            long=True,
        )
        pair = gather_start(own_block)
        input_in.extend([own_block, pair, gather_end(pair)])
        return late

    place = functools.partial(place_kernel, seq_len)
    every = jnp.full((1,), count_img, jnp.int32)
    placed = []

    def place_all():
        placed.extend(
            local(place, [(images.shape, BF)], image_count, out_pair, out_far, perm, smem=(0,))
        )
        placed.extend(
            local(place, [(images.shape, F32)], every, *input_in[1:], perm, smem=(0,))
        )
        return placed

    place = functools.partial(place_kernel, seq_len)
    every = jnp.full((1,), count_img, jnp.int32)
    done = []

    def meanwhile():
        (total,) = local(add_kernel, [pack], grad, after(came_near, input_in[1]))
        grad_up, grad_down = local(
            weight_out_kernel,
            [((1,) + expert_up.shape[1:], F32), ((1,) + expert_down.shape[1:], F32)],
            core,
            grad,
            came_near,
            swap_cores(total),
            smem=(0,),
        )
        done.extend(
            local(place, [(images.shape, BF)], image_count, out_pair, out_far, perm, smem=(0,))
        )
        done.extend(
            local(place, [(images.shape, F32)], every, *input_in[1:], perm, smem=(0,))
        )
        done.extend([grad_up, grad_down])
        return done

    dense, peer = sum_groups(dense, other, input_of, meanwhile)
    block_output, input_grad, grad_up, grad_down = done
    late_shape = (round_up(spare + 1, 16), width)
    grad_qkv, grad_proj, late = local(
        dense_out_kernel,
        [(qkv_weight.shape[::-1], F32), (proj_weight.shape, F32), (late_shape, F32)],
        core,
        dense,
        peer,
        smem=(0,),
    )
    return (
        block_output,
        input_grad,
        late[0],
        grad_qkv.T,
        grad_proj,
        late[1],
        late[2 : 1 + spare].T,
        grad_up,
        grad_down,
    )


def solution(mesh):
    placed = (
        P(("expert", "dp"), None, None),
        P(("expert", "dp"), None, None),
        P(("expert", "dp")),
        P(("expert", "dp"), None, None),
        P(),
        P(None, "tensor"),
        P("tensor", None),
        P(),
        P(),
        P("expert", None, "tensor"),
        P("expert", "tensor", None),
    )
    return jax.shard_map(
        on_device,
        mesh=mesh,
        in_specs=placed,
        out_specs=(
            P(("expert", "dp"), None, None),
            P(("expert", "dp"), None, None),
            P(),
            P(None, "tensor"),
            P("tensor", None),
            P(),
            P(),
            P("expert", None, "tensor"),
            P("expert", "tensor", None),
        ),
        check_vma=False,
    )
```

```python
import functools

import jax
import jax.numpy as jnp
from jax import lax
from jax.experimental import pallas as pl
from jax.experimental.pallas import tpu as pltpu
from jax.sharding import PartitionSpec as P

HD = 64
LANES = 128
LONG = 1 << 36
SPILLS = 10 << 20
epsilon = 1e-06
BF = jnp.bfloat16
F32 = jnp.float32


def round_up(value, step):
    return -(-value // step) * step


def dot(left, right):
    return jnp.dot(left, right, preferred_element_type=F32)


def dot_nt(left, right):
    return lax.dot_general(left, right, (((1,), (1,)), ((), ())), preferred_element_type=F32)


def dot_tn(left, right):
    return lax.dot_general(left, right, (((0,), (0,)), ((), ())), preferred_element_type=F32)


def normalize(values):
    center = values - jnp.mean(values, axis=-1, keepdims=True)
    scale = lax.rsqrt(jnp.mean(center * center, axis=-1, keepdims=True) + epsilon)
    return center * scale, scale


def normalize_back(normal, scale, dnormal):
    mean_d = jnp.mean(dnormal, axis=-1, keepdims=True)
    mean_dn = jnp.mean(dnormal * normal, axis=-1, keepdims=True)
    return scale * (dnormal - mean_d - normal * mean_dn)


def after(value, *others):
    return lax.optimization_barrier((value,) + others)[0]


def local(kernel, outs, *args, scratch=(), smem=(), far=(), long=False):
    apart = [i for group in far for i in group]
    args = [
        pltpu.with_memory_space_constraint(a, pltpu.HBM) if i in apart else a
        for i, a in enumerate(args)
    ]
    shapes = [jax.ShapeDtypeStruct(shape, dtype) for shape, dtype in outs]
    place = lambda i: pltpu.SMEM if i in smem else pltpu.HBM if i in apart else pltpu.VMEM
    groups = [((len(group), *args[group[0]].shape), args[group[0]].dtype) for group in far]
    scratch = [jax.ShapeDtypeStruct(shape, dtype) for shape, dtype in (*scratch, *groups)]
    held = [*shapes, *scratch, *(a for i, a in enumerate(args) if i not in apart)]
    size = sum(a.size * a.dtype.itemsize for a in held)
    scratch = [pltpu.VMEM(a.shape, a.dtype) for a in scratch]
    scratch += [pltpu.SemaphoreType.DMA((len(group),)) for group in far]
    return pl.pallas_call(
        kernel,
        out_shape=shapes,
        in_specs=[pl.BlockSpec(memory_space=place(i)) for i in range(len(args))],
        out_specs=[pl.BlockSpec(memory_space=pltpu.VMEM)] * len(outs),
        scratch_shapes=scratch,
        compiler_params=pltpu.CompilerParams(vmem_limit_bytes=min(size + SPILLS, 60 << 20)),
        cost_estimate=pl.CostEstimate(
            flops=LONG if long else 0, bytes_accessed=0, transcendentals=0
        ),
    )(*args)


def spread(rows, columns, step):
    row = lax.broadcasted_iota(jnp.int32, (rows, columns), 0)
    column = lax.broadcasted_iota(jnp.int32, (rows, columns), 1)
    if step:
        row, column = column, row
    same = (row >> 6 == column >> 7) & ((row & 63) == (column & 127))
    return same.astype(F32).astype(BF)


def fetch(sources, held, sems):
    for i, source in enumerate(sources):
        pltpu.make_async_copy(source, held.at[i], sems.at[i]).start()


def fetched(held, sems, i):
    pltpu.make_async_copy(held.at[i], held.at[i], sems.at[i]).wait()


def pack_kernel(core_ref, up_far, down_far, mine_ref, other_ref, sent_ref, held, sems):
    fetch([up_far, down_far], held, sems)
    width, half = held.shape[2], held.shape[3] // 2
    fetched(held, sems, 1)
    down_t = held[1, 0].T
    fetched(held, sems, 0)
    first = core_ref[0] == 0

    def put(mine, other):
        for ref, at in ((mine_ref, mine), (sent_ref, mine), (other_ref, other)):
            ref[:width] = held[0, 0, :, at : at + half]
            ref[width:] = down_t[:, at : at + half]

    @pl.when(first)
    def _():
        put(0, half)

    @pl.when(jnp.logical_not(first))
    def _():
        put(half, 0)


def put_blocks(refs, value):
    rows = refs[0].shape[0]
    for s, ref in enumerate(refs):
        ref[...] = value[s * rows : (s + 1) * rows]


def put_parts(refs, value):
    rows = refs[0].shape[0]
    refs[0][...] = value[:rows]
    refs[1][...] = value[rows : 2 * rows]
    refs[2][...] = value[2 * rows :]


def route_kernel(seq_len, count_ref, deal_row, rows_ref, cot_ref, perm, up_own, disp_all, *refs):
    ups, held = refs[:-1], refs[-1]
    seq_pad = held.shape[0] // cot_ref.shape[0]
    own = up_own.shape[0]
    hit = lax.broadcasted_iota(jnp.int32, perm.shape, 0) == deal_row[...]
    perm[...] = hit.astype(F32).astype(BF)
    held[...] = jnp.zeros_like(held)
    for image in range(cot_ref.shape[0]):
        keep = (count_ref[0] > image).astype(F32)
        at = image * seq_pad
        held[at : at + seq_len] = cot_ref[image].astype(F32) * keep
    place = lax.broadcasted_iota(jnp.int32, disp_all.shape, 0)
    hit = (place == rows_ref[0:1]) | (place == rows_ref[1:2])
    disp = hit.astype(F32).astype(BF)
    disp_all[...] = disp
    upstream = held[...].astype(BF)
    put_blocks(ups, dot(disp, upstream).astype(BF))
    up_own[...] = dot(perm[:own], upstream).astype(BF)


def qkv_kernel(seq_len, x_ref, gain, weight_t, normed, wide_t, qkv, x_pad, held):
    seq_pad = held.shape[0] // x_ref.shape[0]
    held[...] = jnp.zeros_like(held)
    for image in range(x_ref.shape[0]):
        held[image * seq_pad : image * seq_pad + seq_len] = x_ref[image].astype(F32)
    values = held[...]
    x_pad[...] = values.astype(BF)
    normal, _ = normalize(values)
    low = (normal * gain[...]).astype(BF)
    normed[...] = low
    wide_low = dot(spread(wide_t.shape[0], weight_t.shape[0], True), weight_t[...]).astype(BF)
    wide_t[...] = wide_low
    qkv[...] = dot_nt(low, wide_low).astype(BF)


def pieces(qkv, rows, head):
    at = lambda c: qkv[rows, (head * 3 + c) * LANES : (head * 3 + c + 1) * LANES]
    return at(0), at(1), at(2)


def softmax_of(queries, keys, seq_len):
    scores = dot_nt(queries, keys) * 0.125
    real = lax.broadcasted_iota(jnp.int32, scores.shape, 1) < seq_len
    scores = jnp.where(real, scores, -1e30)
    exps = jnp.exp(scores - jnp.max(scores, axis=-1, keepdims=True))
    return exps / jnp.sum(exps, axis=-1, keepdims=True)


def attend_kernel(seq_len, count_img, qkv, perm, proj, att, *refs):
    parts, held = refs[:-1], refs[-1]
    heads = qkv.shape[1] // (3 * LANES)
    seq_pad = qkv.shape[0] // count_img
    for image in range(count_img):
        rows = slice(image * seq_pad, (image + 1) * seq_pad)
        for head in range(heads):
            queries, keys, values = pieces(qkv, rows, head)
            probs = softmax_of(queries, keys, seq_len).astype(BF)
            held[rows, head * LANES : (head + 1) * LANES] = dot(probs, values).astype(BF)
    att_perm = dot(perm[...], held[...]).astype(BF)
    att[...] = att_perm
    wide = dot(spread(held.shape[1], proj.shape[0], True), proj[...]).astype(BF)
    put_parts(parts, dot(att_perm, wide).astype(BF))


def mix_kernel(part, first, second, x_pad, perm, gain, disp_all, residual, x_own, disp, *outs):
    own = part.shape[0]
    perm_own = perm[:own]
    own_x = dot(perm_own, x_pad[...])
    x_own[...] = own_x.astype(BF)
    own_disp = dot_nt(disp_all[...], perm_own).astype(BF)
    disp[...] = own_disp
    attn = part[...].astype(F32) + first[:own].astype(F32)
    whole = own_x + (attn + second[...].astype(F32))
    residual[...] = whole
    normal, _ = normalize(whole)
    put_blocks(outs, dot(own_disp, (normal * gain[...]).astype(BF)).astype(BF))


def gelu_parts(hidden):
    size = jnp.abs(hidden)
    density = jnp.exp(-0.5 * (hidden * hidden))
    t = 1.0 / (1.0 + (0.3275911 * 0.5**0.5) * size)
    poly = 0.5 * 1.061405429 * t - 0.5 * 1.453152027
    poly = poly * t + 0.5 * 1.421413741
    poly = poly * t - 0.5 * 0.284496736
    poly = poly * t + 0.5 * 0.254829592
    tail = poly * t * density
    cdf = jnp.where(hidden < 0.0, tail, 1.0 - tail)
    return cdf, cdf + hidden * density * 0.3989422804014327


def expert_kernel(blocks, packs, last, columns, *refs):
    refs = list(refs)
    take = lambda n: [refs.pop(0) for _ in range(n)]
    rows_refs, up_refs, pack_refs = take(blocks), take(blocks), take(packs)
    router, mark = take(2)
    earlier = take(4 if columns else 2) if last else None
    up_held, pack_held, up_sems, pack_sems = refs[-4:]
    refs = refs[:-4]
    fetch(up_refs, up_held, up_sems)
    fetch(pack_refs, pack_held, pack_sems)
    rows = jnp.concatenate([r[...] for r in rows_refs], axis=0)
    experts = mark.shape[0]
    logits = dot_nt(rows, router[...])
    lane = lax.broadcasted_iota(jnp.int32, logits.shape, 1)
    logits = jnp.where(lane < experts, logits, -1e30)
    exps = jnp.exp(logits - jnp.max(logits, axis=-1, keepdims=True))
    gates = exps / jnp.sum(exps, axis=-1, keepdims=True)
    onehot = mark[0:1]
    gate = jnp.sum(gates * onehot, axis=1, keepdims=True)
    for i in range(blocks):
        fetched(up_held, up_sems, i)
    upstream = up_held[...].reshape(rows.shape).astype(F32)
    dout = (gate * upstream).astype(BF)
    if last:
        backs, mixtures = take(blocks), take(blocks)
        dlog_t, *kept, active, dhidden, acc, dacc = refs
        acc[...], dacc[...] = earlier[0][...], earlier[1][...]
    else:
        acc, dacc, active, dhidden, dout_ref = refs
        dout_ref[...] = dout
        acc[...] = jnp.zeros_like(acc)
        dacc[...] = jnp.zeros_like(dacc)
    half, width = pack_held.shape[2], pack_held.shape[1] // 2

    def step(p, carry):
        fetched(pack_held, pack_sems, p)
        up, down_t = pack_held[p, :width], pack_held[p, width:]
        at = pl.ds(pl.multiple_of(p * half, half), half)
        hidden = dot(rows, up)
        cdf, slope = gelu_parts(hidden)
        low = (hidden * cdf).astype(BF)
        active[:, at] = low
        dlow = (dot(dout, down_t) * slope).astype(BF)
        dhidden[:, at] = dlow
        acc[...] += dot_nt(low, down_t)
        dacc[...] += dot_nt(dlow, up)
        return carry

    lax.fori_loop(0, packs, step, 0)
    if last:
        out_rows = acc[...].astype(BF).astype(F32)
        put_blocks(mixtures, (gate * out_rows).astype(BF))
        dgate = jnp.sum(upstream * out_rows, axis=1, keepdims=True)
        dlog = (gates * dgate * (onehot - gate)).astype(BF)
        put_blocks(backs, (dacc[...] + dot(dlog, router[...])).astype(BF))
        dlog_t[...] = dot_tn(dlog, rows)
        if columns:
            lists = ((earlier[2], earlier[3]), (active, dhidden))
            weight_grads(rows, dout, lists, columns, *kept)


def weight_grads(rows, dout, lists, columns, keep, sent):
    half, width = keep.shape[2], rows.shape[1]
    rows_t, dout_t = rows.T, dout.T
    for i, (call, place) in enumerate(columns):
        target = (sent, keep)[i // 2]
        active, dhidden = lists[call]
        at = slice(place * half, (place + 1) * half)
        target[i % 2, :width] = dot(rows_t, dhidden[:, at]).astype(BF)
        target[i % 2, width:] = dot(dout_t, active[:, at]).astype(BF)


def weight_kernel(blocks, columns, *refs):
    refs = list(refs)
    rows = jnp.concatenate([refs.pop(0)[...] for _ in range(blocks)], axis=0)
    *lists, dout, keep, sent = refs
    lists = [lists[i : i + 2] for i in range(0, len(lists), 2)]
    weight_grads(rows, dout[...], lists, columns, keep, sent)


def add_kernel(*refs):
    total = refs[0][...].astype(F32)
    for ref in refs[1:-1]:
        total = total + ref[...].astype(F32)
    refs[-1][...] = total.astype(refs[-1].dtype)


def add_parts_kernel(kept, came, first, second, *outs):
    for part, other in enumerate((first, second)):
        total = kept[part].astype(F32) + came[part].astype(F32) + other[...].astype(F32)
        outs[part][...] = total.astype(BF)


def add_split_kernel(*refs):
    total = refs[0][...].astype(F32)
    for ref in refs[1:-2]:
        total = total + ref[...].astype(F32)
    refs[-2][...] = total[0].astype(BF)
    refs[-1][...] = total[1].astype(BF)


def combine_kernel(blocks, used, experts, *refs):
    refs = list(refs)
    back = jnp.concatenate([refs.pop(0)[...] for _ in range(blocks)], axis=0)
    disp, residual, up_own, gain, dlog_t, dresidual, dattn = refs
    dmixed = dot_tn(disp[...], back)
    normal, scale = normalize(residual[...])
    grad_ln2 = jnp.sum(dmixed * normal, axis=0, keepdims=True)
    total = up_own[...].astype(F32) + normalize_back(normal, scale, dmixed * gain[...])
    dresidual[...] = total
    row = lax.broadcasted_iota(jnp.int32, (total.shape[0], 1), 0)
    total = jnp.where(row < used, total, 0.0)
    total = total + jnp.where(row == used, grad_ln2, 0.0)
    for e in range(experts):
        total = total + jnp.where(row == used + 1 + e, dlog_t[e : e + 1], 0.0)
    dattn[...] = total.astype(BF)


def attend_back_kernel(seq_len, count_img, used, *refs):
    pair, far, qkv, x_ref, perm, proj, wide_t, dqkv, *dns, held = refs
    dattn = jnp.concatenate([pair[...], far[...]], axis=0)
    heads = qkv.shape[1] // (3 * LANES)
    seq_pad = qkv.shape[0] // count_img
    wide_proj = dot(spread(heads * LANES, proj.shape[0], True), proj[...]).astype(BF)
    datt = dot_nt(dattn, wide_proj).astype(BF)
    held[...] = dot_tn(perm[...], datt).astype(BF)
    for image in range(count_img):
        rows = slice(image * seq_pad, (image + 1) * seq_pad)
        for head in range(heads):
            queries, keys, values = pieces(qkv, rows, head)
            probs = softmax_of(queries, keys, seq_len)
            d_out = held[rows, head * LANES : (head + 1) * LANES]
            dprobs = dot_nt(d_out, values)
            dscores = probs * (dprobs - jnp.sum(probs * dprobs, axis=-1, keepdims=True))
            dscores = dscores.astype(BF)
            at = head * 3 * LANES
            dqkv[rows, at : at + LANES] = (dot(dscores, keys) * 0.125).astype(BF)
            dqkv[rows, at + LANES : at + 2 * LANES] = (dot_tn(dscores, queries) * 0.125).astype(BF)
            dqkv[rows, at + 2 * LANES : at + 3 * LANES] = dot_tn(probs.astype(BF), d_out).astype(BF)
    dnormed = dot(dqkv[...], wide_t[...])
    normal, _ = normalize(x_ref[...].astype(F32))
    grad_ln1 = jnp.sum(dnormed * normal, axis=0, keepdims=True)
    own = pair.shape[0] // 2
    out = dot(perm[...], dnormed.astype(BF))
    row = lax.broadcasted_iota(jnp.int32, (out.shape[0], 1), 0)
    carries = row == used
    for s in range(1, out.shape[0] // own):
        carries = carries | (row == used + s * own)
    put_parts(dns, (out + jnp.where(carries, grad_ln1, 0.0)).astype(BF))


def dense_kernel(core_ref, pair, far, att, normed, dqkv, mine, *refs):
    others, held = refs[:-1], refs[-1]
    dattn = jnp.concatenate([pair[...], far[...]], axis=0)
    qkv_wide = dot_tn(normed[...], dqkv[...]).astype(BF)
    columns = qkv_wide.shape[1] // 2
    held[:, :columns] = dot(qkv_wide, spread(2 * columns, columns, True))
    proj_wide = dot_tn(dattn, att[...]).astype(BF)
    rows = proj_wide.shape[1] // 2
    held[:, columns:] = dot(proj_wide, spread(2 * rows, rows, True))
    half = mine.shape[0]
    core = core_ref[0]
    mine[...] = held[pl.ds(pl.multiple_of(core * half, half), half)].astype(BF)
    put_blocks(others, held[pl.ds(pl.multiple_of((1 - core) * half, half), half)].astype(BF))


def dense_split_kernel(place_ref, mine, low, high, *refs):
    outs, held = refs[:-1], refs[-1]
    arrived = jnp.concatenate([low[...], high[...]], axis=0)
    held[...] = mine[...].astype(F32) + arrived.astype(F32)
    rows = outs[0].shape[0]
    for s, out in enumerate(outs):
        at = lax.rem(place_ref[0] + s, len(outs)) * rows
        out[...] = held[pl.ds(pl.multiple_of(at, rows), rows)].astype(BF)


def dense_sum_kernel(late, *refs):
    out = refs[-1]
    total = refs[0][...].astype(F32)
    for ref in refs[1:-1]:
        total = total + ref[...].astype(F32)
    rows = total.shape[0]
    out[:rows] = total.astype(BF)
    out[rows:] = late[...].astype(BF)


def dense_join_kernel(place_ref, *refs):
    out, blocks = refs[-1], refs[:-1]
    rows = (out.shape[0] - blocks[0].shape[0]) // (len(blocks) - 1)
    late = jnp.zeros((blocks[0].shape[0] - rows, out.shape[1]), F32)
    for s, block in enumerate(blocks):
        at = lax.rem(place_ref[0] - s + len(blocks), len(blocks)) * rows
        out[pl.ds(pl.multiple_of(at, rows), rows)] = block[:rows]
        late = late + block[rows:].astype(F32)
    out[rows * len(blocks) :] = late.astype(BF)


def dense_out_kernel(core_ref, mine, peer, qkv, proj, late):
    half = qkv.shape[1] // 2
    core = core_ref[0]
    columns = qkv.shape[0]
    late[...] = mine[half:].astype(F32) + peer[half:].astype(F32)

    def put(block, at):
        turned = block[:half].astype(F32).T
        qkv[:, at : at + half] = turned[:columns]
        proj[:, at : at + half] = turned[columns:]

    @pl.when(core == 0)
    def _():
        put(mine[...], 0)
        put(peer[...], half)

    @pl.when(core != 0)
    def _():
        put(peer[...], 0)
        put(mine[...], half)


def add_rows_kernel(mine, arrived, out):
    rows = out.shape[0]
    out[...] = (mine[...].astype(F32) + arrived[rows:].astype(F32)).astype(BF)


def input_kernel(used, spare, dn, first, second, x_own, dresidual, gain, pair, far, out, late):
    own = x_own.shape[0]
    total = dn[...].astype(F32) + first[:own].astype(F32) + second[...].astype(F32)
    normal, scale = normalize(x_own[...].astype(F32))
    back = dresidual[...] + normalize_back(normal, scale, total * gain[...])
    out[...] = back.astype(BF)
    late[...] = jnp.zeros_like(late)
    late[0:1] = total[used : used + 1]
    small = [ref[s * own + used : s * own + used + spare] for ref in (pair, far) for s in range(2)]
    late[1 : 1 + spare] = sum(block.astype(F32) for block in small)


def out_kernel(blocks, *refs):
    mixture = jnp.concatenate([r[...] for r in refs[:blocks]], axis=0)
    disp, residual, out = refs[blocks:]
    out[...] = (residual[...] + dot_tn(disp[...], mixture)).astype(BF)


def place_kernel(seq_len, count_ref, pair, far, perm, out):
    low = jnp.concatenate([pair[...], far[...]], axis=0)
    rows = dot_tn(perm[...], low)
    seq_pad = rows.shape[0] // out.shape[0]
    for image in range(out.shape[0]):
        keep = (count_ref[0] > image).astype(F32)
        block = rows[image * seq_pad : image * seq_pad + seq_len] * keep
        out[image] = block.astype(out.dtype)


def weight_out_kernel(core_ref, mine_ref, arrived_ref, peer_ref, up, down):
    width, half = mine_ref.shape[0] // 2, mine_ref.shape[1]
    mine = mine_ref[...].astype(F32) + arrived_ref[...].astype(F32)
    peer = peer_ref[...].astype(F32)

    def put(block, at):
        up[0, :, at : at + half] = block[:width]
        down[0, at : at + half] = block[width:].T

    @pl.when(core_ref[0] == 0)
    def _():
        put(mine, 0)
        put(peer, half)

    @pl.when(core_ref[0] != 0)
    def _():
        put(peer, 0)
        put(mine, half)


def swap_tensor(block, step):
    size = lax.axis_size("tensor")
    return lax.ppermute(block, "tensor", [(i, i ^ step) for i in range(size)])


def swap_cores(block):
    return lax.ppermute(block, "dp", [(0, 1), (1, 0)])


def swap_by_core(block, first, second):
    size = lax.axis_size("tensor")
    steps = (first, second)
    pairs = [(t * 2 + c, (t ^ steps[c]) * 2 + c) for t in range(size) for c in range(2)]
    return lax.ppermute(block, ("tensor", "dp"), pairs)


def rel_expert(expert):
    size = lax.axis_size("expert")
    if size > 4:
        return expert
    return lax.rem(expert - lax.axis_index("expert") + size, size)


def send_expert(blocks):
    size = lax.axis_size("expert")
    steps = range(1, len(blocks))
    return [
        lax.ppermute(blocks[s], "expert", [(i, (i + s) % size) for i in range(size)]) for s in steps
    ]


def to_experts(blocks, back=False):
    size = lax.axis_size("expert")
    if len(blocks) == 1:
        return [lax.all_to_all(blocks[0], "expert", split_axis=0, concat_axis=0, tiled=True)]
    out = [blocks[0]]
    for step in range(1, size):
        move = -step if back else step
        pairs = [(i, (i + move) % size) for i in range(size)]
        out.append(lax.ppermute(blocks[step], "expert", pairs))
    return out


def gather_start(block):
    return jnp.concatenate([block, swap_by_core(block, 2, 1)], axis=0)


def gather_end(pair):
    return swap_by_core(pair, 1, 2)


def scatter_end(kept, first):
    (sent,) = local(add_rows_kernel, [(kept.shape, BF)], kept, first)
    return swap_by_core(sent, 2, 1), sent


def dense_split(mine, others):
    size = lax.axis_size("expert")
    arrived = [swap_cores(other) for other in others]
    if size > 4:
        return [mine.astype(F32) + jnp.concatenate(arrived, axis=0).astype(F32)]
    half, width = mine.shape
    return local(
        dense_split_kernel,
        [((half // size, width), BF)] * size,
        lax.axis_index("expert")[None],
        mine,
        *arrived,
        scratch=[((half, width), F32)],
        smem=(0,),
    )


def dense_sum(blocks, came, late):
    if len(blocks) == 1:
        return jnp.concatenate(lax.psum((blocks[0], late), "expert"), axis=0).astype(BF)
    shape = (blocks[0].shape[0] + late.shape[0], late.shape[1])
    return local(dense_sum_kernel, [(shape, BF)], late, blocks[0], *came)[0]


def dense_join(total, came, extra):
    if not came:
        return total
    shape = ((total.shape[0] - extra) * (1 + len(came)) + extra, total.shape[1])
    place = lax.axis_index("expert")[None]
    return local(dense_join_kernel, [(shape, BF)], place, total, *came, smem=(0,))[0]


def on_device(
    images,
    cotangent,
    image_count,
    expert_ids,
    ln1_gain,
    qkv_weight,
    proj_weight,
    ln2_gain,
    router_weight,
    expert_up,
    expert_down,
):
    count_img, seq_len, width = images.shape
    tokens = count_img * seq_len
    experts, shares = lax.axis_size("expert"), lax.axis_size("tensor")
    me, my_expert = lax.axis_index("tensor"), lax.axis_index("expert")
    capacity = min(tokens, (2 * tokens // experts // 8 + 2) * 8)
    seq_pad = round_up(seq_len, 16)
    rows_all = count_img * seq_pad
    used = -(-tokens // shares)
    spare = experts + 1
    own = round_up(used + spare, 16)
    cap = min(used, capacity, (capacity + (shares - 1) * (experts - 1)) // shares)
    cap = round_up(cap, 16)
    slots_all = experts * cap
    half = expert_up.shape[2] // 2
    wide = 2 * qkv_weight.shape[1]
    att_width = 2 * proj_weight.shape[0]
    pad = ((0, 0), (0, seq_pad - seq_len), (0, 0))
    core = lax.axis_index("dp")[None]
    gain1, gain2 = ln1_gain[None], ln2_gain[None]

    pack = ((2 * width, half), BF)
    mine, other, sent = local(
        pack_kernel, [pack] * 3, core, expert_up, expert_down, smem=(0,), far=[(1, 2)]
    )
    near = swap_by_core(sent, 1, 2)

    ids = jnp.pad(expert_ids, pad, constant_values=-1).reshape(rows_all, 2)
    index = lax.iota(jnp.int32, rows_all)
    real = lax.rem(index, seq_pad) < seq_len
    pair = jnp.min(ids, axis=1) * experts + jnp.max(ids, axis=1)
    key = jnp.where(real, pair, experts * experts) * 2048 + index
    rank = jnp.sum((key[None, :] < key[:, None]).astype(jnp.int32), axis=1)
    share = jnp.bitwise_xor(lax.rem(rank, shares), me)
    turned = (share & 1) * 2 + (share >> 1)
    share = jnp.where(lax.axis_index("dp") == 0, turned, share)
    deal = jnp.where(real, share * own + rank // shares, -1)
    member = (ids[:, :, None] == lax.iota(jnp.int32, experts)[None, None, :]).astype(F32)
    earlier = ((rank[None, :] < rank[:, None]) & (share[None, :] == 0)).astype(BF)
    counts = dot(earlier, jnp.sum(member, axis=1).astype(BF))
    slots = jnp.sum(member * counts[:, None, :], axis=2).astype(jnp.int32)
    row_of = jnp.where((real & (share == 0))[:, None], rel_expert(ids) * cap + slots, -1)
    parts = 1 if experts > 4 else experts
    block = ((slots_all // parts, width), BF)
    perm, up_own, disp_all, *rows_up = local(
        functools.partial(route_kernel, seq_len),
        [
            ((shares * own, rows_all), BF),
            ((own, width), BF),
            ((slots_all, rows_all), BF),
            *[block] * parts,
        ],
        image_count,
        deal[None],
        row_of.T,
        after(cotangent, mine),
        scratch=[((rows_all, width), F32)],
        smem=(0,),
    )
    rows_up = to_experts(rows_up)

    normed, wide_t, qkv, x = local(
        functools.partial(qkv_kernel, seq_len),
        [((rows_all, width), BF), ((wide, width), BF), ((rows_all, wide), BF), ((rows_all, width), BF)],
        after(images, perm),
        gain1,
        qkv_weight.T,
        scratch=[((rows_all, width), F32)],
    )
    near = after(near, qkv)
    far = [swap_by_core(after(mine, near), 2, 1)]
    rest = [swap_cores(near)]
    share_block = ((own, width), BF)
    share_parts = [share_block, share_block, ((2 * own, width), BF)]
    att, *part = local(
        functools.partial(attend_kernel, seq_len, count_img),
        [((shares * own, att_width), BF), *share_parts],
        qkv,
        perm,
        proj_weight,
        scratch=[((rows_all, att_width), BF)],
    )
    first = swap_by_core(after(part[2], *rows_up), 1, 2)
    rest.append(swap_cores(after(far[0], first)))
    second, sent = scatter_end(after(part[1], far[0]), first)
    far.append(swap_by_core(after(near, first), 2, 1))

    residual, x_own, disp, *sent = local(
        mix_kernel,
        [((own, width), F32), share_block, ((slots_all, own), BF), *[block] * parts],
        part[0],
        after(first, *rest),
        second,
        x,
        perm,
        gain2,
        disp_all,
        long=True,
    )
    rows_in = to_experts(sent)
    rest.append(swap_cores(after(far[1], sent[0])))

    mark = jnp.zeros((experts, LANES), F32).at[:, my_expert].set(1.0)
    router = jnp.pad(router_weight.T, ((0, LANES - experts), (0, 0)))
    packs = [mine, near, far[0], other, *rest[:2]]
    low, full = ((slots_all, width), BF), ((slots_all, width), F32)
    many = lambda packs: ((slots_all, len(packs) * half), BF)
    fetched_at = lambda packs: [
        range(parts, 2 * parts), range(2 * parts, 2 * parts + len(packs))
    ]
    acc, dacc, active, dhidden, dout = local(
        functools.partial(expert_kernel, parts, len(packs), False, ()),
        [full, full, many(packs), many(packs), low],
        *rows_in,
        *rows_up,
        *packs,
        router,
        mark,
        far=fetched_at(packs),
        long=True,
    )
    packs = [far[1], rest[2]]
    two = ((2,) + pack[0], BF)
    columns = ((0, 5), (1, 1), (0, 2), (1, 0))
    fits = parts > 1
    lists = [many(packs), many(packs)]
    results = local(
        functools.partial(expert_kernel, parts, len(packs), True, columns if fits else ()),
        [*[block] * (2 * parts), ((LANES, width), F32), *([two, two] if fits else lists)],
        *rows_in,
        *rows_up,
        *packs,
        router,
        mark,
        acc,
        dacc,
        *([active, dhidden] if fits else []),
        scratch=[*(lists if fits else []), full, full],
        far=fetched_at(packs),
    )
    back = to_experts(list(results[:parts]), True)
    mixture = list(results[parts : 2 * parts])
    dlog_t, keep_b, sent_b = results[2 * parts :]
    if not fits:
        keep_b, sent_b = local(
            functools.partial(weight_kernel, parts, columns),
            [two] * 2,
            *rows_in,
            active,
            dhidden,
            keep_b,
            sent_b,
            dout,
        )
    came_b = swap_cores(sent_b)
    keep_a, sent_a = local(
        functools.partial(weight_kernel, parts, ((0, 3), (0, 4), (0, 0), (0, 1))),
        [two] * 2,
        *rows_in,
        active,
        dhidden,
        after(dout, sent_b),
    )
    came_a = swap_cores(sent_a)
    sum_a, sum_b = local(add_split_kernel, [pack] * 2, keep_b, after(came_b, sent_a))
    came_far_b = swap_by_core(sum_b, 2, 1)

    dresidual, dattn = local(
        functools.partial(combine_kernel, len(back), used, experts),
        [((own, width), F32), share_block],
        after(back[0], came_far_b),
        *back[1:],
        disp,
        residual,
        up_own,
        gain2,
        dlog_t,
        long=True,
    )
    dattn_pair = gather_start(dattn)
    dattn_far = gather_end(dattn_pair)
    came_far_a = swap_by_core(after(sum_a, dattn), 2, 1)
    mixture = to_experts([after(m, dattn) for m in mixture], True)

    dqkv, *dn = local(
        functools.partial(attend_back_kernel, seq_len, count_img, used),
        [(qkv.shape, BF), *share_parts],
        dattn_pair,
        dattn_far,
        after(qkv, came_a),
        x,
        perm,
        proj_weight,
        wide_t,
        scratch=[((rows_all, att_width), BF)],
        long=True,
    )
    first = swap_by_core(dn[2], 1, 2)
    dense, *other = local(
        dense_kernel,
        [((width // 2, width), BF), *[((width // 4, width), BF)] * 2],
        core,
        dattn_pair,
        after(dattn_far, dn[2]),
        att,
        normed,
        dqkv,
        scratch=[((width, width), F32)],
        smem=(0,),
    )
    (out_own,) = local(
        functools.partial(out_kernel, parts), [share_block], *mixture, disp, after(residual, dense)
    )
    out_pair = gather_start(out_own)
    out_far = gather_end(out_pair)
    dense_blocks = dense_split(dense, other)
    dense_came = send_expert(dense_blocks)
    second, sent = scatter_end(after(dn[1], *dense_blocks), first)
    grad, grad_sent = local(
        add_parts_kernel, [pack] * 2, keep_a, came_a, after(came_far_a, sent), came_far_b
    )
    came_near = swap_by_core(grad_sent, 1, 2)
    input_own, late = local(
        functools.partial(input_kernel, used, spare),
        [share_block, ((round_up(spare + 1, 16), width), F32)],
        after(dn[0], grad, out_far, *dense_came),
        first,
        second,
        x_own,
        dresidual,
        gain1,
        dattn_pair,
        dattn_far,
        long=True,
    )
    input_pair = gather_start(input_own)
    dense = dense_sum(dense_blocks, dense_came, late)
    dense_came = send_expert([dense] * len(dense_blocks))
    dense = dense_join(dense, dense_came, late.shape[0])
    peer = swap_cores(dense)
    input_far = gather_end(after(input_pair, dense))
    (total,) = local(add_kernel, [pack], grad, after(came_near, dense))
    total_peer = swap_cores(total)
    place = functools.partial(place_kernel, seq_len)
    (block_output,) = local(
        place, [(images.shape, BF)], image_count, out_pair, out_far, perm, smem=(0,)
    )
    every = jnp.full((1,), count_img, jnp.int32)
    (input_grad,) = local(
        place, [(images.shape, F32)], every, input_pair, input_far, perm, smem=(0,)
    )
    grad_up, grad_down = local(
        weight_out_kernel,
        [((1,) + expert_up.shape[1:], F32), ((1,) + expert_down.shape[1:], F32)],
        core,
        grad,
        came_near,
        after(total_peer, dense),
        smem=(0,),
    )
    late_shape = late.shape
    grad_qkv, grad_proj, late = local(
        dense_out_kernel,
        [(qkv_weight.shape[::-1], F32), (proj_weight.shape, F32), (late_shape, F32)],
        core,
        dense,
        peer,
        smem=(0,),
    )
    return (
        block_output,
        input_grad,
        late[0],
        grad_qkv.T,
        grad_proj,
        late[1],
        late[2 : 1 + spare].T,
        grad_up,
        grad_down,
    )


def solution(mesh):
    placed = (
        P(("expert", "dp"), None, None),
        P(("expert", "dp"), None, None),
        P(("expert", "dp")),
        P(("expert", "dp"), None, None),
        P(),
        P(None, "tensor"),
        P("tensor", None),
        P(),
        P(),
        P("expert", None, "tensor"),
        P("expert", "tensor", None),
    )
    return jax.shard_map(
        on_device,
        mesh=mesh,
        in_specs=placed,
        out_specs=(
            P(("expert", "dp"), None, None),
            P(("expert", "dp"), None, None),
            P(),
            P(None, "tensor"),
            P("tensor", None),
            P(),
            P(),
            P("expert", None, "tensor"),
            P("expert", "tensor", None),
        ),
        check_vma=False,
    )
```

```python
import functools

import jax
import jax.numpy as jnp
from jax import lax
from jax.experimental import pallas as pl
from jax.experimental.pallas import tpu as pltpu
from jax.sharding import PartitionSpec as P

HD = 64
LANES = 128
LONG = 1 << 36
SPILLS = 10 << 20
epsilon = 1e-06
BF = jnp.bfloat16
F32 = jnp.float32


def round_up(value, step):
    return -(-value // step) * step


def dot(left, right):
    return jnp.dot(left, right, preferred_element_type=F32)


def dot_nt(left, right):
    return lax.dot_general(left, right, (((1,), (1,)), ((), ())), preferred_element_type=F32)


def dot_tn(left, right):
    return lax.dot_general(left, right, (((0,), (0,)), ((), ())), preferred_element_type=F32)


def normalize(values):
    center = values - jnp.mean(values, axis=-1, keepdims=True)
    scale = lax.rsqrt(jnp.mean(center * center, axis=-1, keepdims=True) + epsilon)
    return center * scale, scale


def normalize_back(normal, scale, dnormal):
    mean_d = jnp.mean(dnormal, axis=-1, keepdims=True)
    mean_dn = jnp.mean(dnormal * normal, axis=-1, keepdims=True)
    return scale * (dnormal - mean_d - normal * mean_dn)


def after(value, *others):
    return lax.optimization_barrier((value,) + others)[0]


def local(kernel, outs, *args, scratch=(), smem=(), far=(), long=False):
    apart = [i for group in far for i in group]
    args = [
        pltpu.with_memory_space_constraint(a, pltpu.HBM) if i in apart else a
        for i, a in enumerate(args)
    ]
    shapes = [jax.ShapeDtypeStruct(shape, dtype) for shape, dtype in outs]
    place = lambda i: pltpu.SMEM if i in smem else pltpu.HBM if i in apart else pltpu.VMEM
    groups = [((len(group), *args[group[0]].shape), args[group[0]].dtype) for group in far]
    scratch = [jax.ShapeDtypeStruct(shape, dtype) for shape, dtype in (*scratch, *groups)]
    held = [*shapes, *scratch, *(a for i, a in enumerate(args) if i not in apart)]
    size = sum(a.size * a.dtype.itemsize for a in held)
    scratch = [pltpu.VMEM(a.shape, a.dtype) for a in scratch]
    scratch += [pltpu.SemaphoreType.DMA((len(group),)) for group in far]
    return pl.pallas_call(
        kernel,
        out_shape=shapes,
        in_specs=[pl.BlockSpec(memory_space=place(i)) for i in range(len(args))],
        out_specs=[pl.BlockSpec(memory_space=pltpu.VMEM)] * len(outs),
        scratch_shapes=scratch,
        compiler_params=pltpu.CompilerParams(vmem_limit_bytes=min(size + SPILLS, 60 << 20)),
        cost_estimate=pl.CostEstimate(
            flops=LONG if long else 0, bytes_accessed=0, transcendentals=0
        ),
    )(*args)


def spread(rows, columns, step):
    row = lax.broadcasted_iota(jnp.int32, (rows, columns), 0)
    column = lax.broadcasted_iota(jnp.int32, (rows, columns), 1)
    if step:
        row, column = column, row
    same = (row >> 6 == column >> 7) & ((row & 63) == (column & 127))
    return same.astype(F32).astype(BF)


def fetch(sources, held, sems):
    for i, source in enumerate(sources):
        pltpu.make_async_copy(source, held.at[i], sems.at[i]).start()


def fetched(held, sems, i):
    pltpu.make_async_copy(held.at[i], held.at[i], sems.at[i]).wait()


def pack_kernel(core_ref, up_far, down_far, mine_ref, other_ref, sent_ref, held, sems):
    fetch([up_far, down_far], held, sems)
    width, half = held.shape[2], held.shape[3] // 2
    fetched(held, sems, 1)
    down_t = held[1, 0].T
    fetched(held, sems, 0)
    first = core_ref[0] == 0

    def put(mine, other):
        for ref, at in ((mine_ref, mine), (sent_ref, mine), (other_ref, other)):
            ref[:width] = held[0, 0, :, at : at + half]
            ref[width:] = down_t[:, at : at + half]

    @pl.when(first)
    def _():
        put(0, half)

    @pl.when(jnp.logical_not(first))
    def _():
        put(half, 0)


def put_blocks(refs, value):
    rows = refs[0].shape[0]
    for s, ref in enumerate(refs):
        ref[...] = value[s * rows : (s + 1) * rows]


def put_parts(refs, value):
    rows = refs[0].shape[0]
    refs[0][...] = value[:rows]
    refs[1][...] = value[rows : 2 * rows]
    refs[2][...] = value[2 * rows :]


def route_kernel(seq_len, count_ref, deal_row, rows_ref, cot_ref, perm, up_own, disp_all, *refs):
    ups, held = refs[:-1], refs[-1]
    seq_pad = held.shape[0] // cot_ref.shape[0]
    own = up_own.shape[0]
    hit = lax.broadcasted_iota(jnp.int32, perm.shape, 0) == deal_row[...]
    perm[...] = hit.astype(F32).astype(BF)
    held[...] = jnp.zeros_like(held)
    for image in range(cot_ref.shape[0]):
        keep = (count_ref[0] > image).astype(F32)
        at = image * seq_pad
        held[at : at + seq_len] = cot_ref[image].astype(F32) * keep
    place = lax.broadcasted_iota(jnp.int32, disp_all.shape, 0)
    hit = (place == rows_ref[0:1]) | (place == rows_ref[1:2])
    disp = hit.astype(F32).astype(BF)
    disp_all[...] = disp
    upstream = held[...].astype(BF)
    put_blocks(ups, dot(disp, upstream).astype(BF))
    up_own[...] = dot(perm[:own], upstream).astype(BF)


def qkv_kernel(seq_len, x_ref, gain, weight_t, normed, wide_t, qkv, x_pad, held):
    seq_pad = held.shape[0] // x_ref.shape[0]
    held[...] = jnp.zeros_like(held)
    for image in range(x_ref.shape[0]):
        held[image * seq_pad : image * seq_pad + seq_len] = x_ref[image].astype(F32)
    values = held[...]
    x_pad[...] = values.astype(BF)
    normal, _ = normalize(values)
    low = (normal * gain[...]).astype(BF)
    normed[...] = low
    wide_low = dot(spread(wide_t.shape[0], weight_t.shape[0], True), weight_t[...]).astype(BF)
    wide_t[...] = wide_low
    qkv[...] = dot_nt(low, wide_low).astype(BF)


def pieces(qkv, rows, head):
    at = lambda c: qkv[rows, (head * 3 + c) * LANES : (head * 3 + c + 1) * LANES]
    return at(0), at(1), at(2)


def softmax_of(queries, keys, seq_len):
    scores = dot_nt(queries, keys) * 0.125
    real = lax.broadcasted_iota(jnp.int32, scores.shape, 1) < seq_len
    scores = jnp.where(real, scores, -1e30)
    exps = jnp.exp(scores - jnp.max(scores, axis=-1, keepdims=True))
    return exps / jnp.sum(exps, axis=-1, keepdims=True)


def attend_kernel(seq_len, count_img, qkv, perm, proj, att, *refs):
    parts, held = refs[:-1], refs[-1]
    heads = qkv.shape[1] // (3 * LANES)
    seq_pad = qkv.shape[0] // count_img
    for image in range(count_img):
        rows = slice(image * seq_pad, (image + 1) * seq_pad)
        for head in range(heads):
            queries, keys, values = pieces(qkv, rows, head)
            probs = softmax_of(queries, keys, seq_len).astype(BF)
            held[rows, head * LANES : (head + 1) * LANES] = dot(probs, values).astype(BF)
    att_perm = dot(perm[...], held[...]).astype(BF)
    att[...] = att_perm
    wide = dot(spread(held.shape[1], proj.shape[0], True), proj[...]).astype(BF)
    put_parts(parts, dot(att_perm, wide).astype(BF))


def mix_kernel(part, first, second, x_pad, perm, gain, disp_all, residual, x_own, disp, *outs):
    own = part.shape[0]
    perm_own = perm[:own]
    own_x = dot(perm_own, x_pad[...])
    x_own[...] = own_x.astype(BF)
    own_disp = dot_nt(disp_all[...], perm_own).astype(BF)
    disp[...] = own_disp
    attn = part[...].astype(F32) + first[:own].astype(F32)
    whole = own_x + (attn + second[...].astype(F32))
    residual[...] = whole
    normal, _ = normalize(whole)
    put_blocks(outs, dot(own_disp, (normal * gain[...]).astype(BF)).astype(BF))


def gelu_parts(hidden):
    size = jnp.abs(hidden)
    density = jnp.exp(-0.5 * (hidden * hidden))
    t = 1.0 / (1.0 + (0.3275911 * 0.5**0.5) * size)
    poly = 0.5 * 1.061405429 * t - 0.5 * 1.453152027
    poly = poly * t + 0.5 * 1.421413741
    poly = poly * t - 0.5 * 0.284496736
    poly = poly * t + 0.5 * 0.254829592
    tail = poly * t * density
    cdf = jnp.where(hidden < 0.0, tail, 1.0 - tail)
    return cdf, cdf + hidden * density * 0.3989422804014327


def expert_kernel(blocks, packs, last, columns, *refs):
    refs = list(refs)
    take = lambda n: [refs.pop(0) for _ in range(n)]
    rows_refs, up_refs, pack_refs = take(blocks), take(blocks), take(packs)
    router, mark = take(2)
    earlier = take(4 if columns else 2) if last else None
    up_held, pack_held, up_sems, pack_sems = refs[-4:]
    refs = refs[:-4]
    fetch(up_refs, up_held, up_sems)
    fetch(pack_refs, pack_held, pack_sems)
    rows = jnp.concatenate([r[...] for r in rows_refs], axis=0)
    experts = mark.shape[0]
    logits = dot_nt(rows, router[...])
    lane = lax.broadcasted_iota(jnp.int32, logits.shape, 1)
    logits = jnp.where(lane < experts, logits, -1e30)
    exps = jnp.exp(logits - jnp.max(logits, axis=-1, keepdims=True))
    gates = exps / jnp.sum(exps, axis=-1, keepdims=True)
    onehot = mark[0:1]
    gate = jnp.sum(gates * onehot, axis=1, keepdims=True)
    for i in range(blocks):
        fetched(up_held, up_sems, i)
    upstream = up_held[...].reshape(rows.shape).astype(F32)
    dout = (gate * upstream).astype(BF)
    if last:
        backs, mixtures = take(blocks), take(blocks)
        dlog_t, *kept, active, dhidden, acc, dacc = refs
        acc[...], dacc[...] = earlier[0][...], earlier[1][...]
    else:
        acc, dacc, active, dhidden, dout_ref = refs
        dout_ref[...] = dout
        acc[...] = jnp.zeros_like(acc)
        dacc[...] = jnp.zeros_like(dacc)
    half, width = pack_held.shape[2], pack_held.shape[1] // 2

    def step(p, carry):
        fetched(pack_held, pack_sems, p)
        up, down_t = pack_held[p, :width], pack_held[p, width:]
        at = pl.ds(pl.multiple_of(p * half, half), half)
        hidden = dot(rows, up)
        cdf, slope = gelu_parts(hidden)
        low = (hidden * cdf).astype(BF)
        active[:, at] = low
        dlow = (dot(dout, down_t) * slope).astype(BF)
        dhidden[:, at] = dlow
        acc[...] += dot_nt(low, down_t)
        dacc[...] += dot_nt(dlow, up)
        return carry

    lax.fori_loop(0, packs, step, 0)
    if last:
        out_rows = acc[...].astype(BF).astype(F32)
        put_blocks(mixtures, (gate * out_rows).astype(BF))
        dgate = jnp.sum(upstream * out_rows, axis=1, keepdims=True)
        dlog = (gates * dgate * (onehot - gate)).astype(BF)
        put_blocks(backs, (dacc[...] + dot(dlog, router[...])).astype(BF))
        dlog_t[...] = dot_tn(dlog, rows)
        if columns:
            lists = ((earlier[2], earlier[3]), (active, dhidden))
            weight_grads(rows, dout, lists, columns, *kept)


def weight_grads(rows, dout, lists, columns, keep, sent):
    half, width = keep.shape[2], rows.shape[1]
    rows_t, dout_t = rows.T, dout.T
    for i, (call, place) in enumerate(columns):
        target = (sent, keep)[i // 2]
        active, dhidden = lists[call]
        at = slice(place * half, (place + 1) * half)
        target[i % 2, :width] = dot(rows_t, dhidden[:, at]).astype(BF)
        target[i % 2, width:] = dot(dout_t, active[:, at]).astype(BF)


def weight_kernel(blocks, columns, *refs):
    refs = list(refs)
    rows = jnp.concatenate([refs.pop(0)[...] for _ in range(blocks)], axis=0)
    *lists, dout, keep, sent = refs
    lists = [lists[i : i + 2] for i in range(0, len(lists), 2)]
    weight_grads(rows, dout[...], lists, columns, keep, sent)


def add_kernel(*refs):
    total = refs[0][...].astype(F32)
    for ref in refs[1:-1]:
        total = total + ref[...].astype(F32)
    refs[-1][...] = total.astype(refs[-1].dtype)


def add_parts_kernel(kept, came, rest, first, *outs):
    width = first.shape[0]
    arrived = (rest[: 2 * width], jnp.concatenate([first[...], rest[2 * width :]], axis=0))
    for part, out in enumerate(outs):
        total = kept[part].astype(F32) + came[part].astype(F32) + arrived[part].astype(F32)
        out[...] = total.astype(BF)


def add_split_kernel(kept, came, first, rest):
    total = kept[...].astype(F32) + came[...].astype(F32)
    width = total.shape[1] // 2
    first[...] = total[1, :width].astype(BF)
    rest[: 2 * width] = total[0].astype(BF)
    rest[2 * width :] = total[1, width:].astype(BF)


def combine_kernel(blocks, used, experts, *refs):
    refs = list(refs)
    back = jnp.concatenate([refs.pop(0)[...] for _ in range(blocks)], axis=0)
    disp, residual, up_own, gain, dlog_t, dresidual, dattn = refs
    dmixed = dot_tn(disp[...], back)
    normal, scale = normalize(residual[...])
    grad_ln2 = jnp.sum(dmixed * normal, axis=0, keepdims=True)
    total = up_own[...].astype(F32) + normalize_back(normal, scale, dmixed * gain[...])
    dresidual[...] = total
    row = lax.broadcasted_iota(jnp.int32, (total.shape[0], 1), 0)
    total = jnp.where(row < used, total, 0.0)
    total = total + jnp.where(row == used, grad_ln2, 0.0)
    for e in range(experts):
        total = total + jnp.where(row == used + 1 + e, dlog_t[e : e + 1], 0.0)
    dattn[...] = total.astype(BF)


def attend_back_kernel(seq_len, count_img, used, *refs):
    pair, far, qkv, x_ref, perm, proj, wide_t, dqkv, *dns, held = refs
    dattn = jnp.concatenate([pair[...], far[...]], axis=0)
    heads = qkv.shape[1] // (3 * LANES)
    seq_pad = qkv.shape[0] // count_img
    wide_proj = dot(spread(heads * LANES, proj.shape[0], True), proj[...]).astype(BF)
    datt = dot_nt(dattn, wide_proj).astype(BF)
    held[...] = dot_tn(perm[...], datt).astype(BF)
    for image in range(count_img):
        rows = slice(image * seq_pad, (image + 1) * seq_pad)
        for head in range(heads):
            queries, keys, values = pieces(qkv, rows, head)
            probs = softmax_of(queries, keys, seq_len)
            d_out = held[rows, head * LANES : (head + 1) * LANES]
            dprobs = dot_nt(d_out, values)
            dscores = probs * (dprobs - jnp.sum(probs * dprobs, axis=-1, keepdims=True))
            dscores = dscores.astype(BF)
            at = head * 3 * LANES
            dqkv[rows, at : at + LANES] = (dot(dscores, keys) * 0.125).astype(BF)
            dqkv[rows, at + LANES : at + 2 * LANES] = (dot_tn(dscores, queries) * 0.125).astype(BF)
            dqkv[rows, at + 2 * LANES : at + 3 * LANES] = dot_tn(probs.astype(BF), d_out).astype(BF)
    dnormed = dot(dqkv[...], wide_t[...])
    normal, _ = normalize(x_ref[...].astype(F32))
    grad_ln1 = jnp.sum(dnormed * normal, axis=0, keepdims=True)
    own = pair.shape[0] // 2
    out = dot(perm[...], dnormed.astype(BF))
    row = lax.broadcasted_iota(jnp.int32, (out.shape[0], 1), 0)
    carries = row == used
    for s in range(1, out.shape[0] // own):
        carries = carries | (row == used + s * own)
    put_parts(dns, (out + jnp.where(carries, grad_ln1, 0.0)).astype(BF))


def dense_kernel(core_ref, pair, far, att, normed, dqkv, mine, *refs):
    others, held = refs[:-1], refs[-1]
    dattn = jnp.concatenate([pair[...], far[...]], axis=0)
    qkv_wide = dot_tn(normed[...], dqkv[...]).astype(BF)
    columns = qkv_wide.shape[1] // 2
    held[:, :columns] = dot(qkv_wide, spread(2 * columns, columns, True))
    proj_wide = dot_tn(dattn, att[...]).astype(BF)
    rows = proj_wide.shape[1] // 2
    held[:, columns:] = dot(proj_wide, spread(2 * rows, rows, True))
    half = mine.shape[0]
    core = core_ref[0]
    mine[...] = held[pl.ds(pl.multiple_of(core * half, half), half)].astype(BF)
    put_blocks(others, held[pl.ds(pl.multiple_of((1 - core) * half, half), half)].astype(BF))


def dense_split_kernel(place_ref, mine, low, high, *refs):
    outs, held = refs[:-1], refs[-1]
    arrived = jnp.concatenate([low[...], high[...]], axis=0)
    held[...] = mine[...].astype(F32) + arrived.astype(F32)
    rows = outs[0].shape[0]
    for s, out in enumerate(outs):
        at = lax.rem(place_ref[0] + s, len(outs)) * rows
        out[...] = held[pl.ds(pl.multiple_of(at, rows), rows)].astype(BF)


def dense_sum_kernel(late, *refs):
    out = refs[-1]
    total = refs[0][...].astype(F32)
    for ref in refs[1:-1]:
        total = total + ref[...].astype(F32)
    rows = total.shape[0]
    out[:rows] = total.astype(BF)
    out[rows:] = late[...].astype(BF)


def dense_join_kernel(place_ref, *refs):
    out, blocks = refs[-1], refs[:-1]
    rows = (out.shape[0] - blocks[0].shape[0]) // (len(blocks) - 1)
    late = jnp.zeros((blocks[0].shape[0] - rows, out.shape[1]), F32)
    for s, block in enumerate(blocks):
        at = lax.rem(place_ref[0] - s + len(blocks), len(blocks)) * rows
        out[pl.ds(pl.multiple_of(at, rows), rows)] = block[:rows]
        late = late + block[rows:].astype(F32)
    out[rows * len(blocks) :] = late.astype(BF)


def dense_out_kernel(core_ref, mine, peer, qkv, proj, late):
    half = qkv.shape[1] // 2
    core = core_ref[0]
    columns = qkv.shape[0]
    late[...] = mine[half:].astype(F32) + peer[half:].astype(F32)

    def put(block, at):
        turned = block[:half].astype(F32).T
        qkv[:, at : at + half] = turned[:columns]
        proj[:, at : at + half] = turned[columns:]

    @pl.when(core == 0)
    def _():
        put(mine[...], 0)
        put(peer[...], half)

    @pl.when(core != 0)
    def _():
        put(peer[...], 0)
        put(mine[...], half)


def add_rows_kernel(mine, arrived, out):
    rows = out.shape[0]
    out[...] = (mine[...].astype(F32) + arrived[rows:].astype(F32)).astype(BF)


def input_kernel(used, spare, dn, first, second, x_own, dresidual, gain, pair, far, out, late):
    own = x_own.shape[0]
    total = dn[...].astype(F32) + first[:own].astype(F32) + second[...].astype(F32)
    normal, scale = normalize(x_own[...].astype(F32))
    back = dresidual[...] + normalize_back(normal, scale, total * gain[...])
    out[...] = back.astype(BF)
    late[...] = jnp.zeros_like(late)
    late[0:1] = total[used : used + 1]
    small = [ref[s * own + used : s * own + used + spare] for ref in (pair, far) for s in range(2)]
    late[1 : 1 + spare] = sum(block.astype(F32) for block in small)


def out_kernel(blocks, *refs):
    mixture = jnp.concatenate([r[...] for r in refs[:blocks]], axis=0)
    disp, residual, out = refs[blocks:]
    out[...] = (residual[...] + dot_tn(disp[...], mixture)).astype(BF)


def place_kernel(seq_len, count_ref, pair, far, perm, out):
    low = jnp.concatenate([pair[...], far[...]], axis=0)
    rows = dot_tn(perm[...], low)
    seq_pad = rows.shape[0] // out.shape[0]
    for image in range(out.shape[0]):
        keep = (count_ref[0] > image).astype(F32)
        block = rows[image * seq_pad : image * seq_pad + seq_len] * keep
        out[image] = block.astype(out.dtype)


def weight_out_kernel(core_ref, mine_ref, arrived_ref, peer_ref, up, down):
    width, half = mine_ref.shape[0] // 2, mine_ref.shape[1]
    mine = mine_ref[...].astype(F32) + arrived_ref[...].astype(F32)
    peer = peer_ref[...].astype(F32)

    def put(block, at):
        up[0, :, at : at + half] = block[:width]
        down[0, at : at + half] = block[width:].T

    @pl.when(core_ref[0] == 0)
    def _():
        put(mine, 0)
        put(peer, half)

    @pl.when(core_ref[0] != 0)
    def _():
        put(peer, 0)
        put(mine, half)


def swap_tensor(block, step):
    size = lax.axis_size("tensor")
    return lax.ppermute(block, "tensor", [(i, i ^ step) for i in range(size)])


def swap_cores(block):
    return lax.ppermute(block, "dp", [(0, 1), (1, 0)])


def swap_by_core(block, first, second):
    size = lax.axis_size("tensor")
    steps = (first, second)
    pairs = [(t * 2 + c, (t ^ steps[c]) * 2 + c) for t in range(size) for c in range(2)]
    return lax.ppermute(block, ("tensor", "dp"), pairs)


def rel_expert(expert):
    size = lax.axis_size("expert")
    if size > 4:
        return expert
    return lax.rem(expert - lax.axis_index("expert") + size, size)


def send_expert(blocks):
    size = lax.axis_size("expert")
    steps = range(1, len(blocks))
    return [
        lax.ppermute(blocks[s], "expert", [(i, (i + s) % size) for i in range(size)]) for s in steps
    ]


def to_experts(blocks, back=False):
    size = lax.axis_size("expert")
    if len(blocks) == 1:
        return [lax.all_to_all(blocks[0], "expert", split_axis=0, concat_axis=0, tiled=True)]
    out = [blocks[0]]
    for step in range(1, size):
        move = -step if back else step
        pairs = [(i, (i + move) % size) for i in range(size)]
        out.append(lax.ppermute(blocks[step], "expert", pairs))
    return out


def gather_start(block):
    return jnp.concatenate([block, swap_by_core(block, 2, 1)], axis=0)


def gather_end(pair):
    return swap_by_core(pair, 1, 2)


def scatter_end(kept, first):
    (sent,) = local(add_rows_kernel, [(kept.shape, BF)], kept, first)
    return swap_by_core(sent, 2, 1), sent


def dense_split(mine, others):
    size = lax.axis_size("expert")
    arrived = [swap_cores(other) for other in others]
    if size > 4:
        return [mine.astype(F32) + jnp.concatenate(arrived, axis=0).astype(F32)]
    half, width = mine.shape
    return local(
        dense_split_kernel,
        [((half // size, width), BF)] * size,
        lax.axis_index("expert")[None],
        mine,
        *arrived,
        scratch=[((half, width), F32)],
        smem=(0,),
    )


def dense_sum(blocks, came, late):
    if len(blocks) == 1:
        return jnp.concatenate(lax.psum((blocks[0], late), "expert"), axis=0).astype(BF)
    shape = (blocks[0].shape[0] + late.shape[0], late.shape[1])
    return local(dense_sum_kernel, [(shape, BF)], late, blocks[0], *came)[0]


def dense_join(total, came, extra):
    if not came:
        return total
    shape = ((total.shape[0] - extra) * (1 + len(came)) + extra, total.shape[1])
    place = lax.axis_index("expert")[None]
    return local(dense_join_kernel, [(shape, BF)], place, total, *came, smem=(0,))[0]


def on_device(
    images,
    cotangent,
    image_count,
    expert_ids,
    ln1_gain,
    qkv_weight,
    proj_weight,
    ln2_gain,
    router_weight,
    expert_up,
    expert_down,
):
    count_img, seq_len, width = images.shape
    tokens = count_img * seq_len
    experts, shares = lax.axis_size("expert"), lax.axis_size("tensor")
    me, my_expert = lax.axis_index("tensor"), lax.axis_index("expert")
    capacity = min(tokens, (2 * tokens // experts // 8 + 2) * 8)
    seq_pad = round_up(seq_len, 16)
    rows_all = count_img * seq_pad
    used = -(-tokens // shares)
    spare = experts + 1
    own = round_up(used + spare, 16)
    cap = min(used, capacity, (capacity + (shares - 1) * (experts - 1)) // shares)
    cap = round_up(cap, 16)
    slots_all = experts * cap
    half = expert_up.shape[2] // 2
    wide = 2 * qkv_weight.shape[1]
    att_width = 2 * proj_weight.shape[0]
    pad = ((0, 0), (0, seq_pad - seq_len), (0, 0))
    core = lax.axis_index("dp")[None]
    gain1, gain2 = ln1_gain[None], ln2_gain[None]

    pack = ((2 * width, half), BF)
    mine, other, sent = local(
        pack_kernel, [pack] * 3, core, expert_up, expert_down, smem=(0,), far=[(1, 2)]
    )
    near = swap_by_core(sent, 1, 2)

    ids = jnp.pad(expert_ids, pad, constant_values=-1).reshape(rows_all, 2)
    index = lax.iota(jnp.int32, rows_all)
    real = lax.rem(index, seq_pad) < seq_len
    pair = jnp.min(ids, axis=1) * experts + jnp.max(ids, axis=1)
    key = jnp.where(real, pair, experts * experts) * 2048 + index
    rank = jnp.sum((key[None, :] < key[:, None]).astype(jnp.int32), axis=1)
    share = jnp.bitwise_xor(lax.rem(rank, shares), me)
    turned = (share & 1) * 2 + (share >> 1)
    share = jnp.where(lax.axis_index("dp") == 0, turned, share)
    deal = jnp.where(real, share * own + rank // shares, -1)
    member = (ids[:, :, None] == lax.iota(jnp.int32, experts)[None, None, :]).astype(F32)
    earlier = ((rank[None, :] < rank[:, None]) & (share[None, :] == 0)).astype(BF)
    counts = dot(earlier, jnp.sum(member, axis=1).astype(BF))
    slots = jnp.sum(member * counts[:, None, :], axis=2).astype(jnp.int32)
    row_of = jnp.where((real & (share == 0))[:, None], rel_expert(ids) * cap + slots, -1)
    parts = 1 if experts > 4 else experts
    block = ((slots_all // parts, width), BF)
    perm, up_own, disp_all, *rows_up = local(
        functools.partial(route_kernel, seq_len),
        [
            ((shares * own, rows_all), BF),
            ((own, width), BF),
            ((slots_all, rows_all), BF),
            *[block] * parts,
        ],
        image_count,
        deal[None],
        row_of.T,
        after(cotangent, mine),
        scratch=[((rows_all, width), F32)],
        smem=(0,),
    )
    rows_up = to_experts(rows_up)

    normed, wide_t, qkv, x = local(
        functools.partial(qkv_kernel, seq_len),
        [((rows_all, width), BF), ((wide, width), BF), ((rows_all, wide), BF), ((rows_all, width), BF)],
        after(images, perm),
        gain1,
        qkv_weight.T,
        scratch=[((rows_all, width), F32)],
    )
    near = after(near, qkv)
    far = [swap_by_core(after(mine, near), 2, 1)]
    rest = [swap_cores(near)]
    share_block = ((own, width), BF)
    share_parts = [share_block, share_block, ((2 * own, width), BF)]
    att, *part = local(
        functools.partial(attend_kernel, seq_len, count_img),
        [((shares * own, att_width), BF), *share_parts],
        qkv,
        perm,
        proj_weight,
        scratch=[((rows_all, att_width), BF)],
    )
    first = swap_by_core(after(part[2], *rows_up), 1, 2)
    rest.append(swap_cores(after(far[0], first)))
    second, sent = scatter_end(after(part[1], far[0]), first)
    far.append(swap_by_core(after(near, first), 2, 1))

    residual, x_own, disp, *sent = local(
        mix_kernel,
        [((own, width), F32), share_block, ((slots_all, own), BF), *[block] * parts],
        part[0],
        after(first, *rest),
        second,
        x,
        perm,
        gain2,
        disp_all,
        long=True,
    )
    rows_in = to_experts(sent)
    rest.append(swap_cores(after(far[1], sent[0])))

    lanes = lax.broadcasted_iota(jnp.int32, (experts, LANES), 1)
    mark = (lanes == my_expert).astype(F32)
    router = jnp.pad(router_weight.T, ((0, LANES - experts), (0, 0)))
    packs = [mine, near, far[0], other, *rest[:2]]
    low, full = ((slots_all, width), BF), ((slots_all, width), F32)
    many = lambda packs: ((slots_all, len(packs) * half), BF)
    fetched_at = lambda packs: [
        range(parts, 2 * parts), range(2 * parts, 2 * parts + len(packs))
    ]
    acc, dacc, active, dhidden, dout = local(
        functools.partial(expert_kernel, parts, len(packs), False, ()),
        [full, full, many(packs), many(packs), low],
        *rows_in,
        *rows_up,
        *packs,
        router,
        mark,
        far=fetched_at(packs),
        long=True,
    )
    packs = [far[1], rest[2]]
    two = ((2,) + pack[0], BF)
    columns = ((0, 5), (1, 1), (0, 2), (1, 0))
    fits = parts > 1
    lists = [many(packs), many(packs)]
    results = local(
        functools.partial(expert_kernel, parts, len(packs), True, columns if fits else ()),
        [*[block] * (2 * parts), ((LANES, width), F32), *([two, two] if fits else lists)],
        *rows_in,
        *rows_up,
        *packs,
        router,
        mark,
        acc,
        dacc,
        *([active, dhidden] if fits else []),
        scratch=[*(lists if fits else []), full, full],
        far=fetched_at(packs),
    )
    back = to_experts(list(results[:parts]), True)
    mixture = list(results[parts : 2 * parts])
    dlog_t, keep_b, sent_b = results[2 * parts :]
    if not fits:
        keep_b, sent_b = local(
            functools.partial(weight_kernel, parts, columns),
            [two] * 2,
            *rows_in,
            active,
            dhidden,
            keep_b,
            sent_b,
            dout,
        )
    came_b = swap_cores(sent_b)
    keep_a, sent_a = local(
        functools.partial(weight_kernel, parts, ((0, 3), (0, 4), (0, 0), (0, 1))),
        [two] * 2,
        *rows_in,
        active,
        dhidden,
        after(dout, sent_b),
    )
    came_a = swap_cores(sent_a)
    sum_b, sum_a = local(
        add_split_kernel,
        [((width, half), BF), ((3 * width, half), BF)],
        keep_b,
        after(came_b, sent_a),
    )
    came_far_b = swap_by_core(sum_b, 2, 1)

    dresidual, dattn = local(
        functools.partial(combine_kernel, len(back), used, experts),
        [((own, width), F32), share_block],
        after(back[0], sum_b),
        *back[1:],
        disp,
        residual,
        up_own,
        gain2,
        dlog_t,
        long=True,
    )
    dattn_pair = gather_start(dattn)
    dattn_far = gather_end(after(dattn_pair, came_far_b))
    came_far_a = swap_by_core(after(sum_a, dattn), 2, 1)
    mixture = to_experts([after(m, dattn) for m in mixture], True)

    dqkv, *dn = local(
        functools.partial(attend_back_kernel, seq_len, count_img, used),
        [(qkv.shape, BF), *share_parts],
        dattn_pair,
        dattn_far,
        after(qkv, came_a),
        x,
        perm,
        proj_weight,
        wide_t,
        scratch=[((rows_all, att_width), BF)],
        long=True,
    )
    first = swap_by_core(dn[2], 1, 2)
    dense, *other = local(
        dense_kernel,
        [((width // 2, width), BF), *[((width // 4, width), BF)] * 2],
        core,
        dattn_pair,
        after(dattn_far, dn[2]),
        att,
        normed,
        dqkv,
        scratch=[((width, width), F32)],
        smem=(0,),
    )
    (out_own,) = local(
        functools.partial(out_kernel, parts), [share_block], *mixture, disp, after(residual, dn[2])
    )
    out_pair = gather_start(out_own)
    dense_blocks = dense_split(dense, other)
    out_far = gather_end(after(out_pair, *dense_blocks))
    dense_came = send_expert(dense_blocks)
    second, sent = scatter_end(dn[1], first)
    grad, grad_sent = local(
        add_parts_kernel, [pack] * 2, keep_a, came_a, after(came_far_a, sent), came_far_b
    )
    came_near = swap_by_core(grad_sent, 1, 2)
    input_own, late = local(
        functools.partial(input_kernel, used, spare),
        [share_block, ((round_up(spare + 1, 16), width), F32)],
        after(dn[0], grad, out_far, *dense_came),
        first,
        second,
        x_own,
        dresidual,
        gain1,
        dattn_pair,
        dattn_far,
        long=True,
    )
    input_pair = gather_start(input_own)
    dense = dense_sum(dense_blocks, dense_came, late)
    dense_came = send_expert([dense] * len(dense_blocks))
    dense = dense_join(after(dense, input_pair), dense_came, late.shape[0])
    peer = swap_cores(dense)
    input_far = gather_end(after(input_pair, dense))
    (total,) = local(add_kernel, [pack], grad, after(came_near, dense))
    total_peer = swap_cores(total)
    place = functools.partial(place_kernel, seq_len)
    (block_output,) = local(
        place, [(images.shape, BF)], image_count, out_pair, out_far, perm, smem=(0,)
    )
    grad_up, grad_down = local(
        weight_out_kernel,
        [((1,) + expert_up.shape[1:], F32), ((1,) + expert_down.shape[1:], F32)],
        core,
        grad,
        came_near,
        after(total_peer, dense),
        smem=(0,),
    )
    late_shape = late.shape
    grad_qkv, grad_proj, late = local(
        dense_out_kernel,
        [(qkv_weight.shape[::-1], F32), (proj_weight.shape, F32), (late_shape, F32)],
        core,
        dense,
        peer,
        smem=(0,),
    )
    every = jnp.full((1,), count_img, jnp.int32)
    (input_grad,) = local(
        place, [(images.shape, F32)], every, input_pair, input_far, after(perm, grad_up, grad_qkv, block_output), smem=(0,)
    )
    return (
        block_output,
        input_grad,
        late[0],
        grad_qkv.T,
        grad_proj,
        late[1],
        late[2 : 1 + spare].T,
        grad_up,
        grad_down,
    )


def solution(mesh):
    placed = (
        P(("expert", "dp"), None, None),
        P(("expert", "dp"), None, None),
        P(("expert", "dp")),
        P(("expert", "dp"), None, None),
        P(),
        P(None, "tensor"),
        P("tensor", None),
        P(),
        P(),
        P("expert", None, "tensor"),
        P("expert", "tensor", None),
    )
    return jax.shard_map(
        on_device,
        mesh=mesh,
        in_specs=placed,
        out_specs=(
            P(("expert", "dp"), None, None),
            P(("expert", "dp"), None, None),
            P(),
            P(None, "tensor"),
            P("tensor", None),
            P(),
            P(),
            P("expert", None, "tensor"),
            P("expert", "tensor", None),
        ),
        check_vma=False,
    )
```

```python
import functools

import jax
import jax.numpy as jnp
from jax import lax
from jax.experimental import pallas as pl
from jax.experimental.pallas import tpu as pltpu
from jax.sharding import PartitionSpec as P

HD = 64
LANES = 128
LONG = 1 << 36
SPILLS = 10 << 20
epsilon = 1e-06
BF = jnp.bfloat16
F32 = jnp.float32


def round_up(value, step):
    return -(-value // step) * step


def dot(left, right):
    return jnp.dot(left, right, preferred_element_type=F32)


def dot_nt(left, right):
    return lax.dot_general(left, right, (((1,), (1,)), ((), ())), preferred_element_type=F32)


def dot_tn(left, right):
    return lax.dot_general(left, right, (((0,), (0,)), ((), ())), preferred_element_type=F32)


def normalize(values):
    center = values - jnp.mean(values, axis=-1, keepdims=True)
    scale = lax.rsqrt(jnp.mean(center * center, axis=-1, keepdims=True) + epsilon)
    return center * scale, scale


def normalize_back(normal, scale, dnormal):
    mean_d = jnp.mean(dnormal, axis=-1, keepdims=True)
    mean_dn = jnp.mean(dnormal * normal, axis=-1, keepdims=True)
    return scale * (dnormal - mean_d - normal * mean_dn)


def after(value, *others):
    return lax.optimization_barrier((value,) + others)[0]


def local(kernel, outs, *args, scratch=(), smem=(), far=(), long=False):
    apart = [i for group in far for i in group]
    args = [
        pltpu.with_memory_space_constraint(a, pltpu.HBM) if i in apart else a
        for i, a in enumerate(args)
    ]
    shapes = [jax.ShapeDtypeStruct(shape, dtype) for shape, dtype in outs]
    place = lambda i: pltpu.SMEM if i in smem else pltpu.HBM if i in apart else pltpu.VMEM
    groups = [((len(group), *args[group[0]].shape), args[group[0]].dtype) for group in far]
    scratch = [jax.ShapeDtypeStruct(shape, dtype) for shape, dtype in (*scratch, *groups)]
    held = [*shapes, *scratch, *(a for i, a in enumerate(args) if i not in apart)]
    size = sum(a.size * a.dtype.itemsize for a in held)
    scratch = [pltpu.VMEM(a.shape, a.dtype) for a in scratch]
    scratch += [pltpu.SemaphoreType.DMA((len(group),)) for group in far]
    return pl.pallas_call(
        kernel,
        out_shape=shapes,
        in_specs=[pl.BlockSpec(memory_space=place(i)) for i in range(len(args))],
        out_specs=[pl.BlockSpec(memory_space=pltpu.VMEM)] * len(outs),
        scratch_shapes=scratch,
        compiler_params=pltpu.CompilerParams(vmem_limit_bytes=min(size + SPILLS, 60 << 20)),
        cost_estimate=pl.CostEstimate(
            flops=LONG if long else 0, bytes_accessed=0, transcendentals=0
        ),
    )(*args)


def spread(rows, columns, step):
    row = lax.broadcasted_iota(jnp.int32, (rows, columns), 0)
    column = lax.broadcasted_iota(jnp.int32, (rows, columns), 1)
    if step:
        row, column = column, row
    same = (row >> 6 == column >> 7) & ((row & 63) == (column & 127))
    return same.astype(F32).astype(BF)


def fetch(sources, held, sems):
    for i, source in enumerate(sources):
        pltpu.make_async_copy(source, held.at[i], sems.at[i]).start()


def fetched(held, sems, i):
    pltpu.make_async_copy(held.at[i], held.at[i], sems.at[i]).wait()


def pack_kernel(core_ref, up_far, down_far, mine_ref, other_ref, held, sems):
    fetch([up_far, down_far], held, sems)
    width, half = held.shape[2], held.shape[3] // 2
    fetched(held, sems, 1)
    down_t = held[1, 0].T
    fetched(held, sems, 0)
    first = core_ref[0] == 0

    def put(mine, other):
        for ref, at in ((mine_ref, mine), (other_ref, other)):
            ref[:width] = held[0, 0, :, at : at + half]
            ref[width:] = down_t[:, at : at + half]

    @pl.when(first)
    def _():
        put(0, half)

    @pl.when(jnp.logical_not(first))
    def _():
        put(half, 0)


def put_blocks(refs, value):
    rows = refs[0].shape[0]
    for s, ref in enumerate(refs):
        ref[...] = value[s * rows : (s + 1) * rows]


def put_parts(refs, value):
    rows = refs[0].shape[0]
    refs[0][...] = value[:rows]
    refs[1][...] = value[rows : 2 * rows]
    refs[2][...] = value[2 * rows :]


def route_kernel(seq_len, count_ref, deal_row, rows_ref, cot_ref, perm, up_own, disp_all, *refs):
    ups, held = refs[:-1], refs[-1]
    seq_pad = held.shape[0] // cot_ref.shape[0]
    own = up_own.shape[0]
    hit = lax.broadcasted_iota(jnp.int32, perm.shape, 0) == deal_row[...]
    perm[...] = hit.astype(F32).astype(BF)
    held[...] = jnp.zeros_like(held)
    for image in range(cot_ref.shape[0]):
        keep = (count_ref[0] > image).astype(F32)
        at = image * seq_pad
        held[at : at + seq_len] = cot_ref[image].astype(F32) * keep
    place = lax.broadcasted_iota(jnp.int32, disp_all.shape, 0)
    hit = (place == rows_ref[0:1]) | (place == rows_ref[1:2])
    disp = hit.astype(F32).astype(BF)
    disp_all[...] = disp
    upstream = held[...].astype(BF)
    put_blocks(ups, dot(disp, upstream).astype(BF))
    up_own[...] = dot(perm[:own], upstream).astype(BF)


def qkv_kernel(seq_len, x_ref, gain, weight_t, normed, wide_t, qkv, x_pad, held):
    seq_pad = held.shape[0] // x_ref.shape[0]
    held[...] = jnp.zeros_like(held)
    for image in range(x_ref.shape[0]):
        held[image * seq_pad : image * seq_pad + seq_len] = x_ref[image].astype(F32)
    values = held[...]
    x_pad[...] = values.astype(BF)
    normal, _ = normalize(values)
    low = (normal * gain[...]).astype(BF)
    normed[...] = low
    wide_low = dot(spread(wide_t.shape[0], weight_t.shape[0], True), weight_t[...]).astype(BF)
    wide_t[...] = wide_low
    qkv[...] = dot_nt(low, wide_low).astype(BF)


def pieces(qkv, rows, head):
    at = lambda c: qkv[rows, (head * 3 + c) * LANES : (head * 3 + c + 1) * LANES]
    return at(0), at(1), at(2)


def softmax_of(queries, keys, seq_len):
    scores = dot_nt(queries, keys) * 0.125
    real = lax.broadcasted_iota(jnp.int32, scores.shape, 1) < seq_len
    scores = jnp.where(real, scores, -1e30)
    exps = jnp.exp(scores - jnp.max(scores, axis=-1, keepdims=True))
    return exps / jnp.sum(exps, axis=-1, keepdims=True)


def attend_kernel(seq_len, count_img, qkv, perm, proj, att, *refs):
    parts, held = refs[:-1], refs[-1]
    heads = qkv.shape[1] // (3 * LANES)
    seq_pad = qkv.shape[0] // count_img
    for image in range(count_img):
        rows = slice(image * seq_pad, (image + 1) * seq_pad)
        for head in range(heads):
            queries, keys, values = pieces(qkv, rows, head)
            probs = softmax_of(queries, keys, seq_len).astype(BF)
            held[rows, head * LANES : (head + 1) * LANES] = dot(probs, values).astype(BF)
    att_perm = dot(perm[...], held[...]).astype(BF)
    att[...] = att_perm
    wide = dot(spread(held.shape[1], proj.shape[0], True), proj[...]).astype(BF)
    put_parts(parts, dot(att_perm, wide).astype(BF))


def mix_kernel(part, first, second, x_pad, perm, gain, disp_all, residual, x_own, disp, *outs):
    own = part.shape[0]
    perm_own = perm[:own]
    own_x = dot(perm_own, x_pad[...])
    x_own[...] = own_x.astype(BF)
    own_disp = dot_nt(disp_all[...], perm_own).astype(BF)
    disp[...] = own_disp
    attn = part[...].astype(F32) + first[:own].astype(F32)
    whole = own_x + (attn + second[...].astype(F32))
    residual[...] = whole
    normal, _ = normalize(whole)
    put_blocks(outs, dot(own_disp, (normal * gain[...]).astype(BF)).astype(BF))


def gelu_parts(hidden):
    size = jnp.abs(hidden)
    density = jnp.exp(-0.5 * (hidden * hidden))
    t = 1.0 / (1.0 + (0.3275911 * 0.5**0.5) * size)
    poly = 0.5 * 1.061405429 * t - 0.5 * 1.453152027
    poly = poly * t + 0.5 * 1.421413741
    poly = poly * t - 0.5 * 0.284496736
    poly = poly * t + 0.5 * 0.254829592
    tail = poly * t * density
    cdf = jnp.where(hidden < 0.0, tail, 1.0 - tail)
    return cdf, cdf + hidden * density * 0.3989422804014327


def expert_kernel(blocks, packs, last, columns, *refs):
    refs = list(refs)
    take = lambda n: [refs.pop(0) for _ in range(n)]
    rows_refs, up_refs, pack_refs = take(blocks), take(blocks), take(packs)
    router, mark = take(2)
    earlier = take(4 if columns else 2) if last else None
    up_held, pack_held, up_sems, pack_sems = refs[-4:]
    refs = refs[:-4]
    fetch(up_refs, up_held, up_sems)
    fetch(pack_refs, pack_held, pack_sems)
    rows = jnp.concatenate([r[...] for r in rows_refs], axis=0)
    experts = mark.shape[0]
    logits = dot_nt(rows, router[...])
    lane = lax.broadcasted_iota(jnp.int32, logits.shape, 1)
    logits = jnp.where(lane < experts, logits, -1e30)
    exps = jnp.exp(logits - jnp.max(logits, axis=-1, keepdims=True))
    gates = exps / jnp.sum(exps, axis=-1, keepdims=True)
    onehot = mark[0:1]
    gate = jnp.sum(gates * onehot, axis=1, keepdims=True)
    for i in range(blocks):
        fetched(up_held, up_sems, i)
    upstream = up_held[...].reshape(rows.shape).astype(F32)
    dout = (gate * upstream).astype(BF)
    if last:
        backs, mixtures = take(blocks), take(blocks)
        dlog_t, *kept, active, dhidden, acc, dacc = refs
        acc[...], dacc[...] = earlier[0][...], earlier[1][...]
    else:
        acc, dacc, active, dhidden, dout_ref = refs
        dout_ref[...] = dout
        acc[...] = jnp.zeros_like(acc)
        dacc[...] = jnp.zeros_like(dacc)
    half, width = pack_held.shape[2], pack_held.shape[1] // 2

    def step(p, carry):
        fetched(pack_held, pack_sems, p)
        up, down_t = pack_held[p, :width], pack_held[p, width:]
        at = pl.ds(pl.multiple_of(p * half, half), half)
        hidden = dot(rows, up)
        cdf, slope = gelu_parts(hidden)
        low = (hidden * cdf).astype(BF)
        active[:, at] = low
        dlow = (dot(dout, down_t) * slope).astype(BF)
        dhidden[:, at] = dlow
        acc[...] += dot_nt(low, down_t)
        dacc[...] += dot_nt(dlow, up)
        return carry

    lax.fori_loop(0, packs, step, 0)
    if last:
        out_rows = acc[...].astype(BF).astype(F32)
        put_blocks(mixtures, (gate * out_rows).astype(BF))
        dgate = jnp.sum(upstream * out_rows, axis=1, keepdims=True)
        dlog = (gates * dgate * (onehot - gate)).astype(BF)
        put_blocks(backs, (dacc[...] + dot(dlog, router[...])).astype(BF))
        dlog_t[...] = dot_tn(dlog, rows)
        if columns:
            lists = ((earlier[2], earlier[3]), (active, dhidden))
            weight_grads(rows, dout, lists, columns, *kept)


def weight_grads(rows, dout, lists, columns, keep, sent):
    half, width = keep.shape[2], rows.shape[1]
    rows_t, dout_t = rows.T, dout.T
    for i, (call, place) in enumerate(columns):
        target = (sent, keep)[i // 2]
        active, dhidden = lists[call]
        at = slice(place * half, (place + 1) * half)
        target[i % 2, :width] = dot(rows_t, dhidden[:, at]).astype(BF)
        target[i % 2, width:] = dot(dout_t, active[:, at]).astype(BF)


def weight_kernel(blocks, columns, *refs):
    refs = list(refs)
    rows = jnp.concatenate([refs.pop(0)[...] for _ in range(blocks)], axis=0)
    *lists, dout, keep, sent = refs
    lists = [lists[i : i + 2] for i in range(0, len(lists), 2)]
    weight_grads(rows, dout[...], lists, columns, keep, sent)


def add_kernel(*refs):
    total = refs[0][...].astype(F32)
    for ref in refs[1:-1]:
        total = total + ref[...].astype(F32)
    refs[-1][...] = total.astype(refs[-1].dtype)


def add_parts_kernel(kept, came, rest, first, *outs):
    width = first.shape[0]
    arrived = (rest[: 2 * width], jnp.concatenate([first[...], rest[2 * width :]], axis=0))
    for part, out in enumerate(outs):
        total = kept[part].astype(F32) + came[part].astype(F32) + arrived[part].astype(F32)
        out[...] = total.astype(BF)


def add_split_kernel(kept, came, first, rest):
    total = kept[...].astype(F32) + came[...].astype(F32)
    width = total.shape[1] // 2
    first[...] = total[1, :width].astype(BF)
    rest[: 2 * width] = total[0].astype(BF)
    rest[2 * width :] = total[1, width:].astype(BF)


def combine_kernel(blocks, used, experts, *refs):
    refs = list(refs)
    back = jnp.concatenate([refs.pop(0)[...] for _ in range(blocks)], axis=0)
    disp, residual, up_own, gain, dlog_t, dresidual, dattn = refs
    dmixed = dot_tn(disp[...], back)
    normal, scale = normalize(residual[...])
    grad_ln2 = jnp.sum(dmixed * normal, axis=0, keepdims=True)
    total = up_own[...].astype(F32) + normalize_back(normal, scale, dmixed * gain[...])
    dresidual[...] = total
    row = lax.broadcasted_iota(jnp.int32, (total.shape[0], 1), 0)
    total = jnp.where(row < used, total, 0.0)
    total = total + jnp.where(row == used, grad_ln2, 0.0)
    for e in range(experts):
        total = total + jnp.where(row == used + 1 + e, dlog_t[e : e + 1], 0.0)
    dattn[...] = total.astype(BF)


def attend_back_kernel(seq_len, count_img, used, *refs):
    pair, far, qkv, x_ref, perm, proj, wide_t, dqkv, *dns, held = refs
    dattn = jnp.concatenate([pair[...], far[...]], axis=0)
    heads = qkv.shape[1] // (3 * LANES)
    seq_pad = qkv.shape[0] // count_img
    wide_proj = dot(spread(heads * LANES, proj.shape[0], True), proj[...]).astype(BF)
    datt = dot_nt(dattn, wide_proj).astype(BF)
    held[...] = dot_tn(perm[...], datt).astype(BF)
    for image in range(count_img):
        rows = slice(image * seq_pad, (image + 1) * seq_pad)
        for head in range(heads):
            queries, keys, values = pieces(qkv, rows, head)
            probs = softmax_of(queries, keys, seq_len)
            d_out = held[rows, head * LANES : (head + 1) * LANES]
            dprobs = dot_nt(d_out, values)
            dscores = probs * (dprobs - jnp.sum(probs * dprobs, axis=-1, keepdims=True))
            dscores = dscores.astype(BF)
            at = head * 3 * LANES
            dqkv[rows, at : at + LANES] = (dot(dscores, keys) * 0.125).astype(BF)
            dqkv[rows, at + LANES : at + 2 * LANES] = (dot_tn(dscores, queries) * 0.125).astype(BF)
            dqkv[rows, at + 2 * LANES : at + 3 * LANES] = dot_tn(probs.astype(BF), d_out).astype(BF)
    dnormed = dot(dqkv[...], wide_t[...])
    normal, _ = normalize(x_ref[...].astype(F32))
    grad_ln1 = jnp.sum(dnormed * normal, axis=0, keepdims=True)
    own = pair.shape[0] // 2
    out = dot(perm[...], dnormed.astype(BF))
    row = lax.broadcasted_iota(jnp.int32, (out.shape[0], 1), 0)
    carries = row == used
    for s in range(1, out.shape[0] // own):
        carries = carries | (row == used + s * own)
    put_parts(dns, (out + jnp.where(carries, grad_ln1, 0.0)).astype(BF))


def dense_kernel(core_ref, pair, far, att, normed, dqkv, mine, *refs):
    others, held = refs[:-1], refs[-1]
    dattn = jnp.concatenate([pair[...], far[...]], axis=0)
    qkv_wide = dot_tn(normed[...], dqkv[...]).astype(BF)
    columns = qkv_wide.shape[1] // 2
    held[:, :columns] = dot(qkv_wide, spread(2 * columns, columns, True))
    proj_wide = dot_tn(dattn, att[...]).astype(BF)
    rows = proj_wide.shape[1] // 2
    held[:, columns:] = dot(proj_wide, spread(2 * rows, rows, True))
    half = mine.shape[0]
    core = core_ref[0]
    mine[...] = held[pl.ds(pl.multiple_of(core * half, half), half)].astype(BF)
    put_blocks(others, held[pl.ds(pl.multiple_of((1 - core) * half, half), half)].astype(BF))


def dense_split_kernel(place_ref, mine, low, high, *refs):
    outs, held = refs[:-1], refs[-1]
    arrived = jnp.concatenate([low[...], high[...]], axis=0)
    held[...] = mine[...].astype(F32) + arrived.astype(F32)
    rows = outs[0].shape[0]
    for s, out in enumerate(outs):
        at = lax.rem(place_ref[0] + s, len(outs)) * rows
        out[...] = held[pl.ds(pl.multiple_of(at, rows), rows)].astype(BF)


def dense_sum_kernel(late, *refs):
    out = refs[-1]
    total = refs[0][...].astype(F32)
    for ref in refs[1:-1]:
        total = total + ref[...].astype(F32)
    rows = total.shape[0]
    out[:rows] = total.astype(BF)
    out[rows:] = late[...].astype(BF)


def dense_join_kernel(place_ref, *refs):
    out, blocks = refs[-1], refs[:-1]
    rows = (out.shape[0] - blocks[0].shape[0]) // (len(blocks) - 1)
    late = jnp.zeros((blocks[0].shape[0] - rows, out.shape[1]), F32)
    for s, block in enumerate(blocks):
        at = lax.rem(place_ref[0] - s + len(blocks), len(blocks)) * rows
        out[pl.ds(pl.multiple_of(at, rows), rows)] = block[:rows]
        late = late + block[rows:].astype(F32)
    out[rows * len(blocks) :] = late.astype(BF)


def dense_out_kernel(core_ref, mine, peer, qkv, proj, late):
    half = qkv.shape[1] // 2
    core = core_ref[0]
    columns = qkv.shape[0]
    late[...] = mine[half:].astype(F32) + peer[half:].astype(F32)

    def put(block, at):
        turned = block[:half].astype(F32).T
        qkv[:, at : at + half] = turned[:columns]
        proj[:, at : at + half] = turned[columns:]

    @pl.when(core == 0)
    def _():
        put(mine[...], 0)
        put(peer[...], half)

    @pl.when(core != 0)
    def _():
        put(peer[...], 0)
        put(mine[...], half)


def add_rows_kernel(mine, arrived, out):
    rows = out.shape[0]
    out[...] = (mine[...].astype(F32) + arrived[rows:].astype(F32)).astype(BF)


def input_kernel(used, spare, dn, first, second, x_own, dresidual, gain, pair, far, out, late):
    own = x_own.shape[0]
    total = dn[...].astype(F32) + first[:own].astype(F32) + second[...].astype(F32)
    normal, scale = normalize(x_own[...].astype(F32))
    back = dresidual[...] + normalize_back(normal, scale, total * gain[...])
    out[...] = back.astype(BF)
    late[...] = jnp.zeros_like(late)
    late[0:1] = total[used : used + 1]
    small = [ref[s * own + used : s * own + used + spare] for ref in (pair, far) for s in range(2)]
    late[1 : 1 + spare] = sum(block.astype(F32) for block in small)


def out_kernel(blocks, *refs):
    mixture = jnp.concatenate([r[...] for r in refs[:blocks]], axis=0)
    disp, residual, out = refs[blocks:]
    out[...] = (residual[...] + dot_tn(disp[...], mixture)).astype(BF)


def place_kernel(seq_len, count_ref, pair, far, perm, out):
    low = jnp.concatenate([pair[...], far[...]], axis=0)
    rows = dot_tn(perm[...], low)
    seq_pad = rows.shape[0] // out.shape[0]
    for image in range(out.shape[0]):
        keep = (count_ref[0] > image).astype(F32)
        block = rows[image * seq_pad : image * seq_pad + seq_len] * keep
        out[image] = block.astype(out.dtype)


def weight_out_kernel(core_ref, mine_ref, arrived_ref, peer_ref, up, down):
    width, half = mine_ref.shape[0] // 2, mine_ref.shape[1]
    mine = mine_ref[...].astype(F32) + arrived_ref[...].astype(F32)
    peer = peer_ref[...].astype(F32)

    def put(block, at):
        up[0, :, at : at + half] = block[:width]
        down[0, at : at + half] = block[width:].T

    @pl.when(core_ref[0] == 0)
    def _():
        put(mine, 0)
        put(peer, half)

    @pl.when(core_ref[0] != 0)
    def _():
        put(peer, 0)
        put(mine, half)


def swap_tensor(block, step):
    size = lax.axis_size("tensor")
    return lax.ppermute(block, "tensor", [(i, i ^ step) for i in range(size)])


def swap_cores(block):
    return lax.ppermute(block, "dp", [(0, 1), (1, 0)])


def swap_by_core(block, first, second):
    size = lax.axis_size("tensor")
    steps = (first, second)
    pairs = [(t * 2 + c, (t ^ steps[c]) * 2 + c) for t in range(size) for c in range(2)]
    return lax.ppermute(block, ("tensor", "dp"), pairs)


def rel_expert(expert):
    size = lax.axis_size("expert")
    if size > 4:
        return expert
    return lax.rem(expert - lax.axis_index("expert") + size, size)


def send_expert(blocks):
    size = lax.axis_size("expert")
    steps = range(1, len(blocks))
    return [
        lax.ppermute(blocks[s], "expert", [(i, (i + s) % size) for i in range(size)]) for s in steps
    ]


def to_experts(blocks, back=False):
    size = lax.axis_size("expert")
    if len(blocks) == 1:
        return [lax.all_to_all(blocks[0], "expert", split_axis=0, concat_axis=0, tiled=True)]
    out = [blocks[0]]
    for step in range(1, size):
        move = -step if back else step
        pairs = [(i, (i + move) % size) for i in range(size)]
        out.append(lax.ppermute(blocks[step], "expert", pairs))
    return out


def gather_start(block):
    return jnp.concatenate([block, swap_by_core(block, 2, 1)], axis=0)


def gather_end(pair):
    return swap_by_core(pair, 1, 2)


def scatter_end(kept, first):
    (sent,) = local(add_rows_kernel, [(kept.shape, BF)], kept, first)
    return swap_by_core(sent, 2, 1), sent


def dense_split(mine, others):
    size = lax.axis_size("expert")
    arrived = [swap_cores(other) for other in others]
    if size > 4:
        return [mine.astype(F32) + jnp.concatenate(arrived, axis=0).astype(F32)]
    half, width = mine.shape
    return local(
        dense_split_kernel,
        [((half // size, width), BF)] * size,
        lax.axis_index("expert")[None],
        mine,
        *arrived,
        scratch=[((half, width), F32)],
        smem=(0,),
    )


def dense_sum(blocks, came, late):
    if len(blocks) == 1:
        return jnp.concatenate(lax.psum((blocks[0], late), "expert"), axis=0).astype(BF)
    shape = (blocks[0].shape[0] + late.shape[0], late.shape[1])
    return local(dense_sum_kernel, [(shape, BF)], late, blocks[0], *came)[0]


def dense_join(total, came, extra):
    if not came:
        return total
    shape = ((total.shape[0] - extra) * (1 + len(came)) + extra, total.shape[1])
    place = lax.axis_index("expert")[None]
    return local(dense_join_kernel, [(shape, BF)], place, total, *came, smem=(0,))[0]


def on_device(
    images,
    cotangent,
    image_count,
    expert_ids,
    ln1_gain,
    qkv_weight,
    proj_weight,
    ln2_gain,
    router_weight,
    expert_up,
    expert_down,
):
    count_img, seq_len, width = images.shape
    tokens = count_img * seq_len
    experts, shares = lax.axis_size("expert"), lax.axis_size("tensor")
    me, my_expert = lax.axis_index("tensor"), lax.axis_index("expert")
    capacity = min(tokens, (2 * tokens // experts // 8 + 2) * 8)
    seq_pad = round_up(seq_len, 16)
    rows_all = count_img * seq_pad
    used = -(-tokens // shares)
    spare = experts + 1
    own = round_up(used + spare, 16)
    cap = min(used, capacity, (capacity + (shares - 1) * (experts - 1)) // shares)
    cap = round_up(cap, 16)
    slots_all = experts * cap
    half = expert_up.shape[2] // 2
    wide = 2 * qkv_weight.shape[1]
    att_width = 2 * proj_weight.shape[0]
    pad = ((0, 0), (0, seq_pad - seq_len), (0, 0))
    core = lax.axis_index("dp")[None]
    gain1, gain2 = ln1_gain[None], ln2_gain[None]

    pack = ((2 * width, half), BF)
    mine, other = local(
        pack_kernel, [pack] * 2, core, expert_up, expert_down, smem=(0,), far=[(1, 2)]
    )
    near = swap_by_core(mine, 1, 2)

    ids = jnp.pad(expert_ids, pad, constant_values=-1).reshape(rows_all, 2)
    index = lax.iota(jnp.int32, rows_all)
    real = lax.rem(index, seq_pad) < seq_len
    pair = jnp.min(ids, axis=1) * experts + jnp.max(ids, axis=1)
    key = jnp.where(real, pair, experts * experts) * 2048 + index
    rank = jnp.sum((key[None, :] < key[:, None]).astype(jnp.int32), axis=1)
    share = jnp.bitwise_xor(lax.rem(rank, shares), me)
    turned = (share & 1) * 2 + (share >> 1)
    share = jnp.where(lax.axis_index("dp") == 0, turned, share)
    deal = jnp.where(real, share * own + rank // shares, -1)
    member = (ids[:, :, None] == lax.iota(jnp.int32, experts)[None, None, :]).astype(F32)
    earlier = ((rank[None, :] < rank[:, None]) & (share[None, :] == 0)).astype(BF)
    counts = dot(earlier, jnp.sum(member, axis=1).astype(BF))
    slots = jnp.sum(member * counts[:, None, :], axis=2).astype(jnp.int32)
    row_of = jnp.where((real & (share == 0))[:, None], rel_expert(ids) * cap + slots, -1)
    parts = 1 if experts > 4 else experts
    block = ((slots_all // parts, width), BF)
    perm, up_own, disp_all, *rows_up = local(
        functools.partial(route_kernel, seq_len),
        [
            ((shares * own, rows_all), BF),
            ((own, width), BF),
            ((slots_all, rows_all), BF),
            *[block] * parts,
        ],
        image_count,
        deal[None],
        row_of.T,
        after(cotangent, mine),
        scratch=[((rows_all, width), F32)],
        smem=(0,),
    )
    rows_up = to_experts(rows_up)

    normed, wide_t, qkv, x = local(
        functools.partial(qkv_kernel, seq_len),
        [((rows_all, width), BF), ((wide, width), BF), ((rows_all, wide), BF), ((rows_all, width), BF)],
        after(images, perm),
        gain1,
        qkv_weight.T,
        scratch=[((rows_all, width), F32)],
    )
    share_block = ((own, width), BF)
    share_parts = [share_block, share_block, ((2 * own, width), BF)]
    att, *part = local(
        functools.partial(attend_kernel, seq_len, count_img),
        [((shares * own, att_width), BF), *share_parts],
        qkv,
        perm,
        proj_weight,
        scratch=[((rows_all, att_width), BF)],
    )
    near = after(near, part[2], *rows_up)
    far = [swap_by_core(after(mine, near), 2, 1)]
    rest = [swap_cores(near)]
    first = swap_by_core(after(part[2], *rows_up), 1, 2)
    second, sent = scatter_end(part[1], first)
    rest.append(swap_cores(after(far[0], sent)))
    far.append(swap_by_core(after(near, first), 2, 1))

    residual, x_own, disp, *sent = local(
        mix_kernel,
        [((own, width), F32), share_block, ((slots_all, own), BF), *[block] * parts],
        part[0],
        after(first, *rest),
        second,
        x,
        perm,
        gain2,
        disp_all,
        long=True,
    )
    rows_in = to_experts(sent)
    rest.append(swap_cores(after(far[1], sent[0])))

    lanes = lax.broadcasted_iota(jnp.int32, (experts, LANES), 1)
    mark = (lanes == my_expert).astype(F32)
    router = jnp.pad(router_weight.T, ((0, LANES - experts), (0, 0)))
    packs = [mine, near, far[0], other, *rest[:2]]
    low, full = ((slots_all, width), BF), ((slots_all, width), F32)
    many = lambda packs: ((slots_all, len(packs) * half), BF)
    fetched_at = lambda packs: [
        range(parts, 2 * parts), range(2 * parts, 2 * parts + len(packs))
    ]
    acc, dacc, active, dhidden, dout = local(
        functools.partial(expert_kernel, parts, len(packs), False, ()),
        [full, full, many(packs), many(packs), low],
        *rows_in,
        *rows_up,
        *packs,
        router,
        mark,
        far=fetched_at(packs),
        long=True,
    )
    packs = [far[1], rest[2]]
    two = ((2,) + pack[0], BF)
    columns = ((0, 5), (1, 1), (0, 2), (1, 0))
    fits = parts > 1
    lists = [many(packs), many(packs)]
    results = local(
        functools.partial(expert_kernel, parts, len(packs), True, columns if fits else ()),
        [*[block] * (2 * parts), ((LANES, width), F32), *([two, two] if fits else lists)],
        *rows_in,
        *rows_up,
        *packs,
        router,
        mark,
        acc,
        dacc,
        *([active, dhidden] if fits else []),
        scratch=[*(lists if fits else []), full, full],
        far=fetched_at(packs),
    )
    back = to_experts(list(results[:parts]), True)
    mixture = list(results[parts : 2 * parts])
    dlog_t, keep_b, sent_b = results[2 * parts :]
    if not fits:
        keep_b, sent_b = local(
            functools.partial(weight_kernel, parts, columns),
            [two] * 2,
            *rows_in,
            active,
            dhidden,
            keep_b,
            sent_b,
            dout,
        )
    came_b = swap_cores(sent_b)
    keep_a, sent_a = local(
        functools.partial(weight_kernel, parts, ((0, 3), (0, 4), (0, 0), (0, 1))),
        [two] * 2,
        *rows_in,
        active,
        dhidden,
        after(dout, sent_b),
    )
    came_a = swap_cores(sent_a)
    sum_b, sum_a = local(
        add_split_kernel,
        [((width, half), BF), ((3 * width, half), BF)],
        keep_b,
        after(came_b, sent_a),
    )
    came_far_b = swap_by_core(sum_b, 2, 1)

    dresidual, dattn = local(
        functools.partial(combine_kernel, len(back), used, experts),
        [((own, width), F32), share_block],
        after(back[0], sum_b),
        *back[1:],
        disp,
        residual,
        up_own,
        gain2,
        dlog_t,
        long=True,
    )
    dattn_pair = gather_start(dattn)
    dattn_far = gather_end(after(dattn_pair, came_far_b))
    came_far_a = swap_by_core(after(sum_a, dattn), 2, 1)
    mixture = to_experts([after(m, dattn) for m in mixture], True)

    dqkv, *dn = local(
        functools.partial(attend_back_kernel, seq_len, count_img, used),
        [(qkv.shape, BF), *share_parts],
        dattn_pair,
        dattn_far,
        after(qkv, came_a),
        x,
        perm,
        proj_weight,
        wide_t,
        scratch=[((rows_all, att_width), BF)],
        long=True,
    )
    first = swap_by_core(dn[2], 1, 2)
    dense, *other = local(
        dense_kernel,
        [((width // 2, width), BF), *[((width // 4, width), BF)] * 2],
        core,
        dattn_pair,
        after(dattn_far, dn[2]),
        att,
        normed,
        dqkv,
        scratch=[((width, width), F32)],
        smem=(0,),
    )
    (out_own,) = local(
        functools.partial(out_kernel, parts), [share_block], *mixture, disp, after(residual, dn[2])
    )
    out_pair = gather_start(out_own)
    dense_blocks = dense_split(dense, other)
    out_far = gather_end(after(out_pair, *dense_blocks))
    dense_came = send_expert(dense_blocks)
    second, sent = scatter_end(dn[1], first)
    grad, grad_sent = local(
        add_parts_kernel, [pack] * 2, keep_a, came_a, after(came_far_a, sent), came_far_b
    )
    came_near = swap_by_core(grad_sent, 1, 2)
    input_own, late = local(
        functools.partial(input_kernel, used, spare),
        [share_block, ((round_up(spare + 1, 16), width), F32)],
        after(dn[0], grad, out_far, *dense_came),
        first,
        second,
        x_own,
        dresidual,
        gain1,
        dattn_pair,
        dattn_far,
        long=True,
    )
    input_pair = gather_start(input_own)
    dense = dense_sum(dense_blocks, dense_came, late)
    dense_came = send_expert([dense] * len(dense_blocks))
    dense = dense_join(after(dense, input_pair), dense_came, late.shape[0])
    peer = swap_cores(dense)
    input_far = gather_end(after(input_pair, dense))
    (total,) = local(add_kernel, [pack], grad, after(came_near, dense))
    total_peer = swap_cores(total)
    place = functools.partial(place_kernel, seq_len)
    (block_output,) = local(
        place, [(images.shape, BF)], image_count, out_pair, out_far, perm, smem=(0,)
    )
    grad_up, grad_down = local(
        weight_out_kernel,
        [((1,) + expert_up.shape[1:], F32), ((1,) + expert_down.shape[1:], F32)],
        core,
        grad,
        came_near,
        after(total_peer, dense),
        smem=(0,),
    )
    late_shape = late.shape
    grad_qkv, grad_proj, late = local(
        dense_out_kernel,
        [(qkv_weight.shape[::-1], F32), (proj_weight.shape, F32), (late_shape, F32)],
        core,
        dense,
        peer,
        smem=(0,),
    )
    every = jnp.full((1,), count_img, jnp.int32)
    (input_grad,) = local(
        place, [(images.shape, F32)], every, input_pair, input_far, after(perm, grad_up, grad_qkv, block_output), smem=(0,)
    )
    return (
        block_output,
        input_grad,
        late[0],
        grad_qkv.T,
        grad_proj,
        late[1],
        late[2 : 1 + spare].T,
        grad_up,
        grad_down,
    )


def solution(mesh):
    placed = (
        P(("expert", "dp"), None, None),
        P(("expert", "dp"), None, None),
        P(("expert", "dp")),
        P(("expert", "dp"), None, None),
        P(),
        P(None, "tensor"),
        P("tensor", None),
        P(),
        P(),
        P("expert", None, "tensor"),
        P("expert", "tensor", None),
    )
    return jax.shard_map(
        on_device,
        mesh=mesh,
        in_specs=placed,
        out_specs=(
            P(("expert", "dp"), None, None),
            P(("expert", "dp"), None, None),
            P(),
            P(None, "tensor"),
            P("tensor", None),
            P(),
            P(),
            P("expert", None, "tensor"),
            P("expert", "tensor", None),
        ),
        check_vma=False,
    )
```
